128 devices in a mesh: expert: 4 (over z), sector: 32 (over y, x, core).
Axes of the slice: x: 4, y: 4, z: 4, core: 2. Of those that a mesh axis runs over, the one named last changes fastest.
Arguments:
- tokens: bfloat16 [65536, 512], P('sector'), may hold values from -6 to 6
- norm_gain: float32 [512], replicated, may hold values from 0.5 to 1.5
- routes: int32 [65536, 2], P('sector'), may hold values from 0 to 63, all different within a row; in each aligned block of 2048 rows (0 to 2047, 2048 to 4095, ...) at most 128 rows name the same one
- gates: float32 [65536, 2], P('sector'), may hold values from 0.2 to 1
- expert_gate: bfloat16 [64, 512, 2048], P('sector', None, 'expert'), may hold values from -0.25 to 0.25
- expert_up: bfloat16 [64, 512, 2048], P('sector', None, 'expert'), may hold values from -0.25 to 0.25
- expert_down: bfloat16 [64, 2048, 512], P('sector', 'expert'), may hold values from -0.125 to 0.125
- shared_gate: bfloat16 [512, 2048], P(None, 'expert'), may hold values from -0.25 to 0.25
- shared_up: bfloat16 [512, 2048], P(None, 'expert'), may hold values from -0.25 to 0.25
- shared_down: bfloat16 [2048, 512], P('expert'), may hold values from -0.125 to 0.125
Outputs:
- mixed: bfloat16 [65536, 512], P('sector', 'expert')
The draws below stay inside these ranges and needn't reach their ends.
Inputs may be any that keep to these rules, and one draw needn't show every extreme that they name: `routes`: the 2 experts of a token differ. Among the tokens of one sector (aligned blocks of 2048 tokens) each expert is named at most 128 times, a bound that some block reaches in each draw.
All inputs are finite; a program needn't handle non-finite values.
Results may differ from the reference program's by a relative error of at most 0.009.
Values may be sent and summed in bfloat16 or wider, within the bound.
No kernel may reach another device: no remote copies, remote signals or barrier semaphores. Data moves between devices by JAX's collectives and lax.ppermute only.
A program may use at most 128 MiB of HBM per device.

```python
import math
import jax
import jax.numpy as jnp
import numpy as np
from jax import lax

D = 512
FF = 2048
SH = 2048
TOP = 2
TOK_DEV = 2048
EXPERTS = 64
CAP = 128
TOKENS = 65536
N_SECTOR = 32


def shard_levels(stream_key, shape, split, least, largest):
    loudness, own = 1.0, jax.random.fold_in(stream_key, 6)
    for axis_at, blocks in split:
        steps = jnp.exp(jax.random.uniform(jax.random.fold_in(own, axis_at), (blocks,), jnp.float32, least / len(split), largest / len(split)))
        loudness = loudness * jnp.repeat(steps, shape[axis_at] // blocks).reshape([-1 if axis == axis_at else 1 for axis in range(len(shape))])
    return loudness


def deal_out(own_key, own, number, rows, number_of, top, most, skew):
    ranking = jax.random.permutation(own_key, number_of)
    packed, common = portions_of(number_of, rows * top, most, skew, True), portions_of(number_of, rows * top, most, skew, False)
    places = jnp.arange(number_of)

    def named(sizes, turn):
        used = int((sizes > 0).sum())
        fixed = max(1, used // 4)
        passed = fixed + (places - fixed + turn * (used - fixed)) % max(1, number_of - fixed)
        return jnp.zeros((number_of,), jnp.int32).at[ranking[jnp.where(places < fixed, places, passed)]].set(jnp.asarray(sizes, jnp.int32))

    sizes = jnp.where(number % 4 == 0, named(packed, number // 4), named(common, number - number // 4 - 1))
    mixed = jax.random.permutation(jax.random.fold_in(own, 3), number_of)
    source_of, sink = mixed[0:number_of // 2 * 2:2], mixed[1:number_of // 2 * 2:2]
    room = jnp.minimum(sizes[source_of] - 1, most - sizes[sink]) // 2
    room = jnp.where((source_of == ranking[0]) | (sink == ranking[0]) | (sizes[sink] == 0), 0, jnp.maximum(room, 0))
    passed = jax.random.randint(jax.random.fold_in(own, 4), (number_of // 2,), 0, 1 << 20) % (room + 1)
    sizes = sizes.at[source_of].add(-passed).at[sink].add(passed)
    labels = jnp.searchsorted(jnp.cumsum(sizes), jnp.arange(rows * top), side="right").astype(jnp.int32)
    table = labels.reshape(top, rows).T
    table = table[jax.random.permutation(jax.random.fold_in(own, 1), rows)]
    turn = jax.random.randint(jax.random.fold_in(own, 2), (rows, 1), 0, top)
    return jnp.take_along_axis(table, (jnp.arange(top)[None, :] + turn) % top, axis=1)


def portions_of(number_of, total, limit, slope, full):
    weights = [(1 << 20) // math.isqrt(rank ** slope) + 1 for rank in range(1, number_of + 1)]
    largest = limit if full else min(limit, max(-(-total // number_of), total * weights[0] // sum(weights)))
    least = 1 if total - largest >= number_of - 1 else 0
    counts, rest = [largest] + [least] * (number_of - 1), total - largest - least * (number_of - 1)
    while rest > 0:
        free = [i for i in range(1, number_of) if counts[i] < largest] or [i for i in range(1, number_of) if counts[i] < limit]
        whole, remaining = sum([weights[i] for i in free]), rest
        for i in free:
            addition = min(limit - counts[i], max(1, remaining * weights[i] // whole), rest)
            counts[i] = counts[i] + addition
            rest = rest - addition
    return np.array(counts)


def normal_values(key, dims, scale, limit, shards=(), kind=jnp.bfloat16):
    result = scale * jax.random.normal(key, dims, jnp.float32)
    if shards:
        result = result * shard_levels(key, dims, shards, -0.22, 0.18)
    return jnp.clip(result, -limit, limit).astype(kind)


def setup_inputs(seed: int = 0) -> dict:
    streams_of = jax.random.split(jax.random.key(seed), 11)
    tokens = normal_values(streams_of[0], (TOKENS, D), 1.0, 6.0, ((0, 32),))
    norm_gain = jnp.clip(1.0 + 0.1 * jax.random.normal(streams_of[1], (D,), jnp.float32), 0.5, 1.5)
    routes_keys = jax.random.split(jax.random.fold_in(streams_of[2], 1), TOKENS // TOK_DEV)
    routes_turns = jax.random.permutation(jax.random.fold_in(streams_of[2], 3), TOKENS // TOK_DEV)
    routes = jax.vmap(lambda own, number: deal_out(jax.random.fold_in(streams_of[2], 2), own, number, TOK_DEV, EXPERTS, TOP, CAP, 2))(routes_keys, routes_turns).reshape((TOKENS, TOP))
    gates = jnp.clip(0.2 + 0.8 * jax.random.uniform(streams_of[3], (TOKENS, TOP), jnp.float32) ** shard_levels(streams_of[3], (TOKENS, TOP), ((0, 32),), -0.2, 0.2), 0.2, 1.0)
    expert_gate = normal_values(streams_of[4], (EXPERTS, D, FF), D ** -0.5, 0.25, ((0, 32), (2, 4)))
    expert_up = normal_values(streams_of[5], (EXPERTS, D, FF), D ** -0.5, 0.25, ((0, 32), (2, 4)))
    expert_down = normal_values(streams_of[6], (EXPERTS, FF, D), FF ** -0.5, 0.125, ((0, 32), (1, 4)))
    shared_gate = normal_values(streams_of[7], (D, SH), D ** -0.5, 0.25, ((1, 4),))
    shared_up = normal_values(streams_of[8], (D, SH), D ** -0.5, 0.25, ((1, 4),))
    shared_down = normal_values(streams_of[9], (SH, D), SH ** -0.5, 0.125, ((0, 4),))
    return {"tokens": tokens, "norm_gain": norm_gain, "routes": routes, "gates": gates, "expert_gate": expert_gate, "expert_up": expert_up, "expert_down": expert_down, "shared_gate": shared_gate, "shared_up": shared_up, "shared_down": shared_down}


def swiglu(rows, w_gate, w_up, w_down):
    gate = jnp.dot(rows, w_gate, preferred_element_type=jnp.float32)
    up = jnp.dot(rows, w_up, preferred_element_type=jnp.float32)
    hidden = (jax.nn.silu(gate) * up).astype(jnp.bfloat16)
    return jnp.dot(hidden, w_down, preferred_element_type=jnp.float32)

def reference(tokens, norm_gain, routes, gates, expert_gate, expert_up, expert_down, shared_gate, shared_up, shared_down):
    values = tokens.astype(jnp.float32)
    scale = lax.rsqrt(lax.optimization_barrier(jnp.mean(values * values, axis=-1, keepdims=True)) + 1e-05)
    normed = (values * scale * norm_gain).astype(jnp.bfloat16)
    shared_out = swiglu(normed, shared_gate, shared_up, shared_down)
    flat = routes.reshape(N_SECTOR, TOK_DEV * TOP).astype(jnp.int32)
    onehot = (flat[:, :, None] == jnp.arange(EXPERTS, dtype=jnp.int32)).astype(jnp.int32)
    rank = lax.optimization_barrier(jnp.sum(jnp.cumsum(onehot, axis=1) * onehot, axis=-1)) - 1
    block = jnp.arange(N_SECTOR, dtype=jnp.int32)[:, None]
    position = ((flat * N_SECTOR + block) * CAP + rank).reshape(-1).astype(jnp.int32)
    rows = jnp.repeat(normed, TOP, axis=0)
    buffer = jnp.zeros((EXPERTS * N_SECTOR * CAP, D), jnp.bfloat16).at[position].set(rows)
    buffer = buffer.reshape(EXPERTS, N_SECTOR * CAP, D)

    def one_expert(operands):
        slots, w_gate, w_up, w_down = operands
        return swiglu(slots, w_gate, w_up, w_down).astype(jnp.bfloat16)
    results = lax.map(one_expert, (buffer, expert_gate, expert_up, expert_down)).reshape(-1, D)
    picked = results[position].astype(jnp.float32).reshape(TOKENS, TOP, D)
    mixed = shared_out + lax.optimization_barrier(jnp.sum(gates[:, :, None] * picked, axis=1))
    return mixed.astype(jnp.bfloat16)
```

```python
import functools

import jax
import jax.numpy as jnp
from jax import lax
from jax.experimental import pallas as pl
from jax.experimental.pallas import tpu as pltpu
from jax.sharding import PartitionSpec as P

F32 = jnp.float32
BF16 = jnp.bfloat16
VMEM_LIMIT = 56 * 1024 * 1024


def dot(a, b):
    return jnp.dot(a, b, preferred_element_type=F32)


def swish(gate, up):
    return (gate / (1.0 + jnp.exp(-gate)) * up).astype(BF16)


def pack_kernel(half, place, gate, up, down, *sends):
    for r, send in enumerate(sends):
        pick = place[0] ^ r
        expert, part = pick // 2, pick % 2
        cols = pl.ds(pl.multiple_of(part * half, half), half)
        for n, w in enumerate((gate, up)):
            send[n, :, :half] = w[expert, :half, cols]
            send[n, :, half:] = w[expert, half:, cols]
        send[2] = down[expert, cols, :]


def pack(gate, up, down, place):
    _, width, hidden = gate.shape
    half = hidden // 2
    shape = jax.ShapeDtypeStruct((3, half, width), BF16)
    return pl.pallas_call(
        functools.partial(pack_kernel, half),
        out_shape=[shape] * 4,
        in_specs=[pl.BlockSpec(memory_space=pltpu.SMEM)] + [pl.BlockSpec(memory_space=pltpu.VMEM)] * 3,
        out_specs=[pl.BlockSpec(memory_space=pltpu.VMEM)] * 4,
        compiler_params=pltpu.CompilerParams(vmem_limit_bytes=VMEM_LIMIT),
        cost_estimate=pl.CostEstimate(flops=0, bytes_accessed=6 * gate.size * 2, transcendentals=0),
    )(place, gate, up, down)


def route_kernel(block, cap, stack, plane, tokens, gain, routes, outgoing, normed, position, chosen):
    step = pl.program_id(0)
    rows, width = tokens.shape
    experts = chosen.shape[0]
    z = plane[0]

    @pl.when(step == 0)
    def _():
        earlier = (
            lax.broadcasted_iota(jnp.int32, (block, block), 0) < lax.broadcasted_iota(jnp.int32, (block, block), 1)
        ).astype(F32).astype(BF16)
        mine = lax.broadcasted_iota(jnp.int32, (experts, block), 0) * stack + z
        column = lax.broadcasted_iota(jnp.int32, (experts, block), 0) * cap
        seen = jnp.zeros((experts, 1), F32)
        for b in range(rows // block):
            at = pl.ds(b * block, block)
            first = routes[0:1, at] == mine
            second = routes[1:2, at] == mine
            named = jnp.where(first | second, 1.0, 0.0).astype(F32)
            rank = dot(named.astype(BF16), earlier) + seen
            chosen[:, at] = jnp.where(first | second, rank, -1.0)
            seen = seen + jnp.sum(named, axis=1, keepdims=True)
            slot = rank + column.astype(F32)
            place = jnp.max(jnp.where(first, slot, -1.0), axis=0, keepdims=True)
            other = jnp.max(jnp.where(second, slot, -1.0), axis=0, keepdims=True)
            position[0:1, at] = place
            position[1:2, at] = other
            values = tokens[at, :].astype(F32)
            scale = lax.rsqrt(jnp.mean(values * values, axis=-1, keepdims=True) + 1e-05)
            normed[at, :] = (values * scale * gain[...]).astype(BF16)

    ranks = lax.broadcasted_iota(jnp.int32, (cap, rows), 0).astype(F32)
    per = outgoing.shape[0] // cap
    masks = [
        jnp.where(ranks == chosen[pl.ds(step * per + i, 1), :], 1.0, 0.0).astype(BF16) for i in range(per)
    ]
    outgoing[...] = dot(jnp.concatenate(masks, axis=0), normed[...]).astype(BF16)


def route(tokens, gain, routes, plane, experts, cap, stack):
    rows, width = tokens.shape
    slots = experts * cap
    block, per = 256, 2 * cap
    return pl.pallas_call(
        functools.partial(route_kernel, block, cap, stack),
        grid=(slots // per,),
        out_shape=[
            jax.ShapeDtypeStruct((slots, width), BF16),
            jax.ShapeDtypeStruct((rows, width), BF16),
            jax.ShapeDtypeStruct((2, rows), F32),
        ],
        in_specs=[
            pl.BlockSpec(memory_space=pltpu.SMEM),
            pl.BlockSpec((rows, width), lambda i: (0, 0)),
            pl.BlockSpec((1, width), lambda i: (0, 0)),
            pl.BlockSpec((2, rows), lambda i: (0, 0)),
        ],
        out_specs=[
            pl.BlockSpec((per, width), lambda i: (i, 0)),
            pl.BlockSpec((rows, width), lambda i: (0, 0)),
            pl.BlockSpec((2, rows), lambda i: (0, 0)),
        ],
        scratch_shapes=[pltpu.VMEM((experts, rows), F32)],
        compiler_params=pltpu.CompilerParams(vmem_limit_bytes=VMEM_LIMIT),
        cost_estimate=pl.CostEstimate(
            flops=2 * slots * rows * width, bytes_accessed=6 * rows * width + 2 * slots * width, transcendentals=rows
        ),
    )(plane, tokens, gain, routes)


def shared_kernel(normed, gate, up, down, out):
    x = normed[...]
    out[...] = dot(swish(dot(x, gate[...]), dot(x, up[...])), down[...])


def shared_expert(normed, gate, up, down):
    rows, width = normed.shape
    hidden = gate.shape[1]
    block = 256
    whole = [pl.BlockSpec(w.shape, lambda i: (0, 0)) for w in (gate, up, down)]
    return pl.pallas_call(
        shared_kernel,
        grid=(rows // block,),
        out_shape=jax.ShapeDtypeStruct((rows, width), F32),
        in_specs=[pl.BlockSpec((block, width), lambda i: (i, 0))] + whole,
        out_specs=pl.BlockSpec((block, width), lambda i: (i, 0)),
        compiler_params=pltpu.CompilerParams(vmem_limit_bytes=VMEM_LIMIT),
        cost_estimate=pl.CostEstimate(
            flops=6 * rows * width * hidden, bytes_accessed=6 * rows * width, transcendentals=rows * hidden
        ),
    )(normed, gate, up, down)


def expert_kernel(slots, *refs):
    weights, out = refs[:-1], refs[-1]
    half = slots.shape[1] // 2
    low, high = slots[:, :half], slots[:, half:]
    total = None
    for w in weights:
        gate = dot(low, w[0, :, :half]) + dot(high, w[0, :, half:])
        up = dot(low, w[1, :, :half]) + dot(high, w[1, :, half:])
        part = dot(swish(gate, up), w[2])
        total = part if total is None else total + part
    out[...] = total.astype(BF16)


def expert(slots, weights):
    rows, width = slots.shape
    block = 256
    hidden = sum(w.shape[1] for w in weights)
    return pl.pallas_call(
        expert_kernel,
        grid=(rows // block,),
        out_shape=jax.ShapeDtypeStruct((rows, width), BF16),
        in_specs=[pl.BlockSpec((block, width), lambda i: (i, 0))]
        + [pl.BlockSpec(w.shape, lambda i: (0, 0, 0)) for w in weights],
        out_specs=pl.BlockSpec((block, width), lambda i: (i, 0)),
        compiler_params=pltpu.CompilerParams(vmem_limit_bytes=VMEM_LIMIT),
        cost_estimate=pl.CostEstimate(
            flops=6 * rows * width * hidden, bytes_accessed=4 * rows * width + 6 * width * hidden,
            transcendentals=rows * hidden,
        ),
    )(slots, *weights)


def combine_kernel(position, gates, back, shared, out):
    slots = back.shape[0]
    rows = shared.shape[0]
    table = jnp.concatenate([position[...], gates[...], jnp.zeros((4, rows), F32)], axis=0).T
    number = lax.broadcasted_iota(jnp.int32, (rows, slots), 1).astype(F32)
    weight = jnp.where(
        number == table[:, 0:1], table[:, 2:3], jnp.where(number == table[:, 1:2], table[:, 3:4], 0.0)
    )
    mixed = (dot(weight.astype(BF16), back[...]) + shared[...]).astype(BF16)
    part = out.shape[2]
    for q in range(out.shape[0]):
        out[q] = mixed[:, q * part : (q + 1) * part]


def combine(position, gates, back, shared, planes):
    rows, width = shared.shape
    slots = back.shape[0]
    block = 256
    return pl.pallas_call(
        combine_kernel,
        grid=(rows // block,),
        out_shape=jax.ShapeDtypeStruct((planes, rows, width // planes), BF16),
        in_specs=[
            pl.BlockSpec((2, block), lambda i: (0, i)),
            pl.BlockSpec((2, block), lambda i: (0, i)),
            pl.BlockSpec((slots, width), lambda i: (0, 0)),
            pl.BlockSpec((block, width), lambda i: (i, 0)),
        ],
        out_specs=pl.BlockSpec((planes, block, width // planes), lambda i: (0, i, 0)),
        compiler_params=pltpu.CompilerParams(vmem_limit_bytes=VMEM_LIMIT),
        cost_estimate=pl.CostEstimate(
            flops=2 * rows * slots * width, bytes_accessed=6 * rows * width + 2 * slots * width, transcendentals=0
        ),
    )(position, gates, back, shared)


def per_device(
    tokens,
    norm_gain,
    routes,
    gates,
    expert_gate,
    expert_up,
    expert_down,
    shared_gate,
    shared_up,
    shared_down,
):
    rows, width = tokens.shape
    planes, sectors = lax.axis_size("expert"), lax.axis_size("sector")
    columns = sectors // 2
    cap = 128
    both = ("expert", "sector")
    z = lax.axis_index("expert").astype(jnp.int32).reshape(1)

    sends = pack(expert_gate, expert_up, expert_down, z)
    weights = []
    for r, send in enumerate(sends):
        moves = []
        for source in range(planes):
            for s in range(sectors):
                pick = source ^ r
                target = 2 * (s % 2) + pick // 2
                moves.append((source * sectors + s, target * sectors + (s // 2) * 2 + pick % 2))
        half = lax.ppermute(send, both, moves)
        other = lax.ppermute(half, "sector", [(s, s ^ 1) for s in range(sectors)])
        weights += [half, other]

    outgoing, normed, position = route(tokens, norm_gain.reshape(1, width), routes.T, z, columns, cap, planes)
    slots = lax.all_to_all(outgoing.reshape(sectors, -1, width), "sector", 0, 0, tiled=True)
    shared = shared_expert(normed, shared_gate, shared_up, shared_down)
    results = expert(slots.reshape(-1, width), weights)
    back = lax.all_to_all(results.reshape(sectors, -1, width), "sector", 0, 0, tiled=True)
    parts = combine(position, gates.T, back.reshape(-1, width), shared, planes)
    parts = lax.all_to_all(parts, "expert", 0, 0, tiled=True)
    return jnp.sum(parts.astype(F32), axis=0).astype(BF16)


def solution(mesh):
    in_specs = (
        P("sector", None),
        P(),
        P("sector", None),
        P("sector", None),
        P("sector", None, "expert"),
        P("sector", None, "expert"),
        P("sector", "expert", None),
        P(None, "expert"),
        P(None, "expert"),
        P("expert", None),
    )
    out_specs = P("sector", "expert")
    return jax.shard_map(
        per_device, mesh=mesh, in_specs=in_specs, out_specs=out_specs, check_vma=False
    )
```

```python
import functools

import jax
import jax.numpy as jnp
from jax import lax
from jax.experimental import pallas as pl
from jax.experimental.pallas import tpu as pltpu
from jax.sharding import PartitionSpec as P

F32 = jnp.float32
BF16 = jnp.bfloat16
VMEM_LIMIT = 56 * 1024 * 1024


def dot(a, b):
    return jnp.dot(a, b, preferred_element_type=F32)


def swish(gate, up):
    half = 0.5 * gate
    return ((half + half * jnp.tanh(half)) * up).astype(BF16)


def pack_kernel(half, place, gate, up, down, *sends):
    for r, send in enumerate(sends):
        pick = place[0] ^ r
        expert, part = pick // 2, pick % 2
        cols = pl.ds(pl.multiple_of(part * half, half), half)
        for n, w in enumerate((gate, up)):
            send[n, :, :half] = w[expert, :half, cols]
            send[n, :, half:] = w[expert, half:, cols]
        send[2] = down[expert, cols, :]


def pack(gate, up, down, place):
    _, width, hidden = gate.shape
    half = hidden // 2
    shape = jax.ShapeDtypeStruct((3, half, width), BF16)
    return pl.pallas_call(
        functools.partial(pack_kernel, half),
        out_shape=[shape] * 4,
        in_specs=[pl.BlockSpec(memory_space=pltpu.SMEM)] + [pl.BlockSpec(memory_space=pltpu.VMEM)] * 3,
        out_specs=[pl.BlockSpec(memory_space=pltpu.VMEM)] * 4,
        compiler_params=pltpu.CompilerParams(vmem_limit_bytes=VMEM_LIMIT),
        cost_estimate=pl.CostEstimate(flops=0, bytes_accessed=6 * gate.size * 2, transcendentals=0),
    )(place, gate, up, down)


def route_kernel(block, cap, stack, plane, tokens, gain, routes, after, outgoing, normed, position, chosen):
    step = pl.program_id(0)
    rows, width = tokens.shape
    experts = chosen.shape[0]
    columns = experts // stack
    per = outgoing.shape[0] // cap

    @pl.when(step == 0)
    def _():
        earlier = (
            lax.broadcasted_iota(jnp.int32, (block, block), 0) < lax.broadcasted_iota(jnp.int32, (block, block), 1)
        ).astype(F32).astype(BF16)
        m = lax.broadcasted_iota(jnp.int32, (experts, block), 0)
        name = (m % columns) * stack + m // columns
        base = (m * cap).astype(F32)
        seen = jnp.zeros((experts, 1), F32)
        for b in range(rows // block):
            at = pl.ds(b * block, block)
            first = routes[0:1, at] == name
            second = routes[1:2, at] == name
            named = jnp.where(first | second, 1.0, 0.0).astype(F32)
            rank = dot(named.astype(BF16), earlier) + seen
            chosen[:, at] = jnp.where(first | second, rank, -1.0)
            seen = seen + jnp.sum(named, axis=1, keepdims=True)
            slot = rank + base
            position[0:1, at] = jnp.max(jnp.where(first, slot, -1.0), axis=0, keepdims=True)
            position[1:2, at] = jnp.max(jnp.where(second, slot, -1.0), axis=0, keepdims=True)
            values = tokens[at, :].astype(F32)
            scale = lax.rsqrt(jnp.mean(values * values, axis=-1, keepdims=True) + 1e-05)
            normed[at, :] = (values * scale * gain[...]).astype(BF16)

    ranks = lax.broadcasted_iota(jnp.int32, (cap, rows), 0).astype(F32)
    start = plane[0] * columns + step * per
    masks = [jnp.where(ranks == chosen[pl.ds(start + i, 1), :], 1.0, 0.0).astype(BF16) for i in range(per)]
    outgoing[...] = dot(jnp.concatenate(masks, axis=0), normed[...]).astype(BF16)


def route(tokens, gain, routes, plane, experts, cap, stack, after):
    rows, width = tokens.shape
    slots = experts // stack * cap
    block, per = 256, 4 * cap
    return pl.pallas_call(
        functools.partial(route_kernel, block, cap, stack),
        grid=(slots // per,),
        out_shape=[
            jax.ShapeDtypeStruct((slots, width), BF16),
            jax.ShapeDtypeStruct((rows, width), BF16),
            jax.ShapeDtypeStruct((2, rows), F32),
        ],
        in_specs=[
            pl.BlockSpec(memory_space=pltpu.SMEM),
            pl.BlockSpec((rows, width), lambda i: (0, 0)),
            pl.BlockSpec((1, width), lambda i: (0, 0)),
            pl.BlockSpec((2, rows), lambda i: (0, 0)),
            pl.BlockSpec(memory_space=pl.ANY),
        ],
        out_specs=[
            pl.BlockSpec((per, width), lambda i: (i, 0)),
            pl.BlockSpec((rows, width), lambda i: (0, 0)),
            pl.BlockSpec((2, rows), lambda i: (0, 0)),
        ],
        scratch_shapes=[pltpu.VMEM((experts, rows), F32)],
        compiler_params=pltpu.CompilerParams(vmem_limit_bytes=VMEM_LIMIT),
        cost_estimate=pl.CostEstimate(
            flops=2 * slots * rows * width, bytes_accessed=6 * rows * width + 2 * slots * width, transcendentals=rows
        ),
    )(plane, tokens, gain, routes, after)


def split_columns(out, values):
    part = out.shape[2]
    for q in range(out.shape[0]):
        out[q] = values[:, q * part : (q + 1) * part]


def shared_kernel(normed, gate, up, down, *rest):
    out = rest[-1]
    x = normed[...]
    split_columns(out, dot(swish(dot(x, gate[...]), dot(x, up[...])), down[...]).astype(BF16))


def shared_expert(normed, gate, up, down, planes, after):
    rows, width = normed.shape
    hidden = gate.shape[1]
    block = 512
    whole = [pl.BlockSpec(w.shape, lambda i: (0, 0)) for w in (gate, up, down)]
    return pl.pallas_call(
        shared_kernel,
        grid=(rows // block,),
        out_shape=jax.ShapeDtypeStruct((planes, rows, width // planes), BF16),
        in_specs=[pl.BlockSpec((block, width), lambda i: (i, 0))] + whole + [pl.BlockSpec(memory_space=pl.ANY)] * len(after),
        out_specs=pl.BlockSpec((planes, block, width // planes), lambda i: (0, i, 0)),
        compiler_params=pltpu.CompilerParams(vmem_limit_bytes=VMEM_LIMIT),
        cost_estimate=pl.CostEstimate(
            flops=60 * rows * width * hidden, bytes_accessed=4 * rows * width, transcendentals=rows * hidden
        ),
    )(normed, gate, up, down, *after)


def expert_kernel(slots, after, *refs):
    weights, (out, w_gate, w_up, w_down, hidden) = refs[:-5], refs[-5:]
    half = slots.shape[1] // 2

    @pl.when(pl.program_id(0) == 0)
    def _():
        for n, w in enumerate(weights):
            at = pl.ds(n * half, half)
            for whole, part in ((w_gate, 0), (w_up, 1)):
                whole[:half, at] = w[part, :, :half]
                whole[half:, at] = w[part, :, half:]
            w_down[at, :] = w[2]

    x = slots[...]
    step = 512
    for n in range(hidden.shape[1] // step):
        at = pl.ds(n * step, step)
        hidden[:, at] = swish(dot(x, w_gate[:, at]), dot(x, w_up[:, at]))
    split_columns(out, dot(hidden[...], w_down[...]).astype(BF16))


def expert(slots, weights, planes, after):
    rows, width = slots.shape
    block = 512
    hidden = sum(w.shape[1] for w in weights)
    return pl.pallas_call(
        expert_kernel,
        grid=(rows // block,),
        out_shape=jax.ShapeDtypeStruct((planes, rows, width // planes), BF16),
        in_specs=[pl.BlockSpec((block, width), lambda i: (i, 0)), pl.BlockSpec(memory_space=pl.ANY)]
        + [pl.BlockSpec(w.shape, lambda i: (0, 0, 0)) for w in weights],
        out_specs=pl.BlockSpec((planes, block, width // planes), lambda i: (0, i, 0)),
        scratch_shapes=[
            pltpu.VMEM((width, hidden), BF16),
            pltpu.VMEM((width, hidden), BF16),
            pltpu.VMEM((hidden, width), BF16),
            pltpu.VMEM((block, hidden), BF16),
        ],
        compiler_params=pltpu.CompilerParams(vmem_limit_bytes=VMEM_LIMIT),
        cost_estimate=pl.CostEstimate(
            flops=6 * rows * width * hidden, bytes_accessed=4 * rows * width + 6 * width * hidden,
            transcendentals=rows * hidden,
        ),
    )(slots, after, *weights)


def combine_kernel(position, gates, back, shared, out, table, total):
    step = pl.program_id(0)
    chunk = back.shape[0]
    rows = out.shape[0]
    block = 512

    @pl.when(step == 0)
    def _():
        for b in range(rows // block):
            at = pl.ds(b * block, block)
            columns = jnp.concatenate([position[:, at], gates[:, at], jnp.zeros((4, block), F32)], axis=0).T
            for n in range(4):
                table[n, at, :] = jnp.broadcast_to(columns[:, n : n + 1], (block, 128))
            total[at, :] = sum(shared[q, at, :].astype(F32) for q in range(shared.shape[0]))

    lane = lax.broadcasted_iota(jnp.int32, (block, 128), 1).astype(F32)
    low = (step * chunk).astype(F32)
    for b in range(rows // block):
        at = pl.ds(b * block, block)
        first, second = table[0, at, :] - low, table[1, at, :] - low
        gate, other = table[2, at, :], table[3, at, :]
        weight = [
            jnp.where(lane + j * 128 == first, gate, jnp.where(lane + j * 128 == second, other, 0.0)).astype(BF16)
            for j in range(chunk // 128)
        ]
        total[at, :] += dot(jnp.concatenate(weight, axis=1), back[...])

    @pl.when(step == pl.num_programs(0) - 1)
    def _():
        out[...] = total[...].astype(BF16)


def combine(position, gates, back, shared):
    planes, rows, part = shared.shape
    slots = back.shape[0]
    chunk = 1024
    return pl.pallas_call(
        combine_kernel,
        grid=(slots // chunk,),
        out_shape=jax.ShapeDtypeStruct((rows, part), BF16),
        in_specs=[
            pl.BlockSpec((2, rows), lambda i: (0, 0)),
            pl.BlockSpec((2, rows), lambda i: (0, 0)),
            pl.BlockSpec((chunk, part), lambda i: (i, 0)),
            pl.BlockSpec((planes, rows, part), lambda i: (0, 0, 0)),
        ],
        out_specs=pl.BlockSpec((rows, part), lambda i: (0, 0)),
        scratch_shapes=[pltpu.VMEM((4, rows, 128), F32), pltpu.VMEM((rows, part), F32)],
        compiler_params=pltpu.CompilerParams(vmem_limit_bytes=VMEM_LIMIT),
        cost_estimate=pl.CostEstimate(
            flops=2 * rows * slots * part, bytes_accessed=10 * rows * part + 2 * slots * part, transcendentals=0
        ),
    )(position, gates, back, shared)


def per_device(
    tokens,
    norm_gain,
    routes,
    gates,
    expert_gate,
    expert_up,
    expert_down,
    shared_gate,
    shared_up,
    shared_down,
):
    rows, width = tokens.shape
    planes, sectors = lax.axis_size("expert"), lax.axis_size("sector")
    columns = sectors // 2
    cap = 128
    both = ("expert", "sector")
    z = lax.axis_index("expert").astype(jnp.int32).reshape(1)

    sends = pack(expert_gate, expert_up, expert_down, z)
    weights = []
    for r, send in enumerate(sends):
        moves = []
        for source in range(planes):
            for s in range(sectors):
                pick = source ^ r
                target = 2 * (s % 2) + pick // 2
                moves.append((source * sectors + s, target * sectors + (s // 2) * 2 + pick % 2))
        half = lax.ppermute(send, both, moves)
        other = lax.ppermute(half, "sector", [(s, s ^ 1) for s in range(sectors)])
        weights += [half, other]

    outgoing, normed, position = route(
        tokens, norm_gain.reshape(1, width), routes.T, z, columns * planes, cap, planes, sends[-1]
    )
    slots = lax.all_to_all(outgoing.reshape(sectors, -1, width), "sector", 0, 0, tiled=True)
    shared = shared_expert(normed, shared_gate, shared_up, shared_down, planes, weights[::2])
    shared_parts = lax.psum_scatter(shared, "expert", scatter_dimension=0, tiled=True)
    results = expert(slots.reshape(-1, width), weights, planes, shared)
    part = width // planes
    back = lax.all_to_all(results.reshape(planes * sectors, -1, part), both, 0, 0, tiled=True)
    return combine(position, gates.T, back.reshape(-1, part), shared_parts)


def solution(mesh):
    in_specs = (
        P("sector", None),
        P(),
        P("sector", None),
        P("sector", None),
        P("sector", None, "expert"),
        P("sector", None, "expert"),
        P("sector", "expert", None),
        P(None, "expert"),
        P(None, "expert"),
        P("expert", None),
    )
    out_specs = P("sector", "expert")
    return jax.shard_map(
        per_device, mesh=mesh, in_specs=in_specs, out_specs=out_specs, check_vma=False
    )
```

```python
import functools

import jax
import jax.numpy as jnp
from jax import lax
from jax.experimental import pallas as pl
from jax.experimental.pallas import tpu as pltpu
from jax.sharding import PartitionSpec as P

F32 = jnp.float32
BF16 = jnp.bfloat16
VMEM_LIMIT = 56 * 1024 * 1024


def dot(a, b):
    return jnp.dot(a, b, preferred_element_type=F32)


def swish(gate, up):
    half = 0.5 * gate
    return ((half + half * jnp.tanh(half)) * up).astype(BF16)


def pack_kernel(half, place, gate, up, down, *sends):
    for r, send in enumerate(sends):
        pick = place[0] ^ r
        expert, part = pick // 2, pick % 2
        cols = pl.ds(pl.multiple_of(part * half, half), half)
        for n, w in enumerate((gate, up)):
            send[n, :, :half] = w[expert, :half, cols]
            send[n, :, half:] = w[expert, half:, cols]
        send[2] = down[expert, cols, :]


def pack(gate, up, down, place):
    _, width, hidden = gate.shape
    half = hidden // 2
    shape = jax.ShapeDtypeStruct((3, half, width), BF16)
    return pl.pallas_call(
        functools.partial(pack_kernel, half),
        out_shape=[shape] * 4,
        in_specs=[pl.BlockSpec(memory_space=pltpu.SMEM)] + [pl.BlockSpec(memory_space=pltpu.VMEM)] * 3,
        out_specs=[pl.BlockSpec(memory_space=pltpu.VMEM)] * 4,
        compiler_params=pltpu.CompilerParams(vmem_limit_bytes=VMEM_LIMIT),
        cost_estimate=pl.CostEstimate(flops=0, bytes_accessed=6 * gate.size * 2, transcendentals=0),
    )(place, gate, up, down)


def route_kernel(block, cap, stack, plane, tokens, gain, routes, after, outgoing, normed, position, chosen):
    step = pl.program_id(0)
    rows, width = tokens.shape
    experts = chosen.shape[0]
    columns = experts // stack
    per = outgoing.shape[0] // cap

    @pl.when(step == 0)
    def _():
        earlier = (
            lax.broadcasted_iota(jnp.int32, (block, block), 0) < lax.broadcasted_iota(jnp.int32, (block, block), 1)
        ).astype(F32).astype(BF16)
        m = lax.broadcasted_iota(jnp.int32, (experts, block), 0)
        name = (m % columns) * stack + m // columns
        base = (m * cap).astype(F32)
        seen = jnp.zeros((experts, 1), F32)
        for b in range(rows // block):
            at = pl.ds(b * block, block)
            first = routes[0:1, at] == name
            second = routes[1:2, at] == name
            named = jnp.where(first | second, 1.0, 0.0).astype(F32)
            rank = dot(named.astype(BF16), earlier) + seen
            chosen[:, at] = jnp.where(first | second, rank, -1.0)
            seen = seen + jnp.sum(named, axis=1, keepdims=True)
            slot = rank + base
            position[0:1, at] = jnp.max(jnp.where(first, slot, -1.0), axis=0, keepdims=True)
            position[1:2, at] = jnp.max(jnp.where(second, slot, -1.0), axis=0, keepdims=True)
            values = tokens[at, :].astype(F32)
            scale = lax.rsqrt(jnp.mean(values * values, axis=-1, keepdims=True) + 1e-05)
            normed[at, :] = (values * scale * gain[...]).astype(BF16)

    ranks = lax.broadcasted_iota(jnp.int32, (cap, rows), 0).astype(F32)
    start = plane[0] * columns + step * per
    masks = [jnp.where(ranks == chosen[pl.ds(start + i, 1), :], 1.0, 0.0).astype(BF16) for i in range(per)]
    outgoing[...] = dot(jnp.concatenate(masks, axis=0), normed[...]).astype(BF16)


def route(tokens, gain, routes, plane, experts, cap, stack, after):
    rows, width = tokens.shape
    slots = experts // stack * cap
    block, per = 256, 4 * cap
    return pl.pallas_call(
        functools.partial(route_kernel, block, cap, stack),
        grid=(slots // per,),
        out_shape=[
            jax.ShapeDtypeStruct((slots, width), BF16),
            jax.ShapeDtypeStruct((rows, width), BF16),
            jax.ShapeDtypeStruct((2, rows), F32),
        ],
        in_specs=[
            pl.BlockSpec(memory_space=pltpu.SMEM),
            pl.BlockSpec((rows, width), lambda i: (0, 0)),
            pl.BlockSpec((1, width), lambda i: (0, 0)),
            pl.BlockSpec((2, rows), lambda i: (0, 0)),
            pl.BlockSpec(memory_space=pl.ANY),
        ],
        out_specs=[
            pl.BlockSpec((per, width), lambda i: (i, 0)),
            pl.BlockSpec((rows, width), lambda i: (0, 0)),
            pl.BlockSpec((2, rows), lambda i: (0, 0)),
        ],
        scratch_shapes=[pltpu.VMEM((experts, rows), F32)],
        compiler_params=pltpu.CompilerParams(vmem_limit_bytes=VMEM_LIMIT),
        cost_estimate=pl.CostEstimate(
            flops=2 * slots * rows * width, bytes_accessed=6 * rows * width + 2 * slots * width, transcendentals=rows
        ),
    )(plane, tokens, gain, routes, after)


def split_columns(out, values):
    part = out.shape[2]
    for q in range(out.shape[0]):
        out[q] = values[:, q * part : (q + 1) * part]


def shared_kernel(plane, normed, gate, up, down, *rest):
    outs, total = rest[:-1], rest[-1]
    x = normed[...]
    total[...] = dot(swish(dot(x, gate[...]), dot(x, up[...])), down[...])
    planes, part = len(outs), outs[0].shape[1]
    for k, out in enumerate(outs):
        target = (plane[0] + k) % planes
        out[...] = total[:, pl.ds(pl.multiple_of(target * part, part), part)].astype(BF16)


def shared_expert(normed, gate, up, down, plane, planes):
    rows, width = normed.shape
    hidden = gate.shape[1]
    block = 512
    part = width // planes
    whole = [pl.BlockSpec(w.shape, lambda i: (0, 0)) for w in (gate, up, down)]
    return pl.pallas_call(
        shared_kernel,
        grid=(rows // block,),
        out_shape=[jax.ShapeDtypeStruct((rows, part), BF16)] * planes,
        in_specs=[pl.BlockSpec(memory_space=pltpu.SMEM), pl.BlockSpec((block, width), lambda i: (i, 0))] + whole,
        out_specs=[pl.BlockSpec((block, part), lambda i: (i, 0))] * planes,
        scratch_shapes=[pltpu.VMEM((block, width), F32)],
        compiler_params=pltpu.CompilerParams(vmem_limit_bytes=VMEM_LIMIT),
        cost_estimate=pl.CostEstimate(
            flops=60 * rows * width * hidden, bytes_accessed=4 * rows * width, transcendentals=rows * hidden
        ),
    )(plane, normed, gate, up, down)


def expert_kernel(slots, after, *refs):
    weights, (out, w_gate, w_up, w_down, hidden) = refs[:-5], refs[-5:]
    half = slots.shape[1] // 2

    @pl.when(pl.program_id(0) == 0)
    def _():
        for n, w in enumerate(weights):
            at = pl.ds(n * half, half)
            for whole, part in ((w_gate, 0), (w_up, 1)):
                whole[:half, at] = w[part, :, :half]
                whole[half:, at] = w[part, :, half:]
            w_down[at, :] = w[2]

    x = slots[...]
    step = 512
    for n in range(hidden.shape[1] // step):
        at = pl.ds(n * step, step)
        hidden[:, at] = swish(dot(x, w_gate[:, at]), dot(x, w_up[:, at]))
    split_columns(out, dot(hidden[...], w_down[...]).astype(BF16))


def expert(slots, weights, planes, after):
    rows, width = slots.shape
    block = 512
    hidden = sum(w.shape[1] for w in weights)
    return pl.pallas_call(
        expert_kernel,
        grid=(rows // block,),
        out_shape=jax.ShapeDtypeStruct((planes, rows, width // planes), BF16),
        in_specs=[pl.BlockSpec((block, width), lambda i: (i, 0)), pl.BlockSpec(memory_space=pl.ANY)]
        + [pl.BlockSpec(w.shape, lambda i: (0, 0, 0)) for w in weights],
        out_specs=pl.BlockSpec((planes, block, width // planes), lambda i: (0, i, 0)),
        scratch_shapes=[
            pltpu.VMEM((width, hidden), BF16),
            pltpu.VMEM((width, hidden), BF16),
            pltpu.VMEM((hidden, width), BF16),
            pltpu.VMEM((block, hidden), BF16),
        ],
        compiler_params=pltpu.CompilerParams(vmem_limit_bytes=VMEM_LIMIT),
        cost_estimate=pl.CostEstimate(
            flops=6 * rows * width * hidden, bytes_accessed=4 * rows * width + 6 * width * hidden,
            transcendentals=rows * hidden,
        ),
    )(slots, after, *weights)


def hold_kernel(*refs):
    pass


def hold(array, *others):
    anywhere = pl.BlockSpec(memory_space=pl.ANY)
    return pl.pallas_call(
        hold_kernel,
        out_shape=jax.ShapeDtypeStruct(array.shape, array.dtype),
        in_specs=[anywhere] * (1 + len(others)),
        out_specs=anywhere,
        input_output_aliases={0: 0},
    )(array, *others)


def combine_kernel(position, gates, back, *refs):
    shared, (out, place, gate, total) = refs[:-4], refs[-4:]
    step = pl.program_id(0)
    chunk = back.shape[0]
    rows = out.shape[0]
    block = 512

    @pl.when(step == 0)
    def _():
        for b in range(rows // block):
            at = pl.ds(b * block, block)
            columns = jnp.concatenate([position[:, at], gates[:, at], jnp.zeros((4, block), F32)], axis=0).T
            for n in range(2):
                place[n, at, :] = jnp.broadcast_to(columns[:, n : n + 1], (block, 128)).astype(jnp.int32).astype(jnp.int16)
                gate[n, at, :] = jnp.broadcast_to(columns[:, n + 2 : n + 3], (block, 128)).astype(BF16)
            total[at, :] = sum(part[at, :].astype(F32) for part in shared)

    lane = lax.broadcasted_iota(jnp.int32, (16, 128), 1) + step * chunk
    numbers = [
        jnp.broadcast_to((lane + j * 128).astype(jnp.int16)[None], (block // 16, 16, 128)).reshape(block, 128)
        for j in range(chunk // 128)
    ]
    for b in range(rows // block):
        at = pl.ds(b * block, block)
        first, second, one, two = place[0, at, :], place[1, at, :], gate[0, at, :], gate[1, at, :]
        weight = [
            jnp.where(number == first, one, jnp.where(number == second, two, jnp.zeros((), BF16))) for number in numbers
        ]
        total[at, :] += dot(jnp.concatenate(weight, axis=1), back[...])

    @pl.when(step == pl.num_programs(0) - 1)
    def _():
        out[...] = total[...].astype(BF16)


def combine(position, gates, back, shared):
    rows, part = shared[0].shape
    slots = back.shape[0]
    chunk = 1024
    return pl.pallas_call(
        combine_kernel,
        grid=(slots // chunk,),
        out_shape=jax.ShapeDtypeStruct((rows, part), BF16),
        in_specs=[
            pl.BlockSpec((2, rows), lambda i: (0, 0)),
            pl.BlockSpec((2, rows), lambda i: (0, 0)),
            pl.BlockSpec((chunk, part), lambda i: (i, 0)),
        ]
        + [pl.BlockSpec((rows, part), lambda i: (0, 0))] * len(shared),
        out_specs=pl.BlockSpec((rows, part), lambda i: (0, 0)),
        scratch_shapes=[
            pltpu.VMEM((2, rows, 128), jnp.int16),
            pltpu.VMEM((2, rows, 128), BF16),
            pltpu.VMEM((rows, part), F32),
        ],
        compiler_params=pltpu.CompilerParams(vmem_limit_bytes=VMEM_LIMIT),
        cost_estimate=pl.CostEstimate(
            flops=2 * rows * slots * part, bytes_accessed=10 * rows * part + 2 * slots * part, transcendentals=0
        ),
    )(position, gates, back, *shared)


def per_device(
    tokens,
    norm_gain,
    routes,
    gates,
    expert_gate,
    expert_up,
    expert_down,
    shared_gate,
    shared_up,
    shared_down,
):
    rows, width = tokens.shape
    planes, sectors = lax.axis_size("expert"), lax.axis_size("sector")
    columns = sectors // 2
    cap = 128
    both = ("expert", "sector")
    z = lax.axis_index("expert").astype(jnp.int32).reshape(1)

    sends = pack(expert_gate, expert_up, expert_down, z)
    weights = []
    for r, send in enumerate(sends):
        moves = []
        for source in range(planes):
            for s in range(sectors):
                pick = source ^ r
                target = 2 * (s % 2) + pick // 2
                moves.append((source * sectors + s, target * sectors + (s // 2) * 2 + pick % 2))
        half = lax.ppermute(send, both, moves)
        other = lax.ppermute(half, "sector", [(s, s ^ 1) for s in range(sectors)])
        weights += [half, other]

    outgoing, normed, position = route(
        tokens, norm_gain.reshape(1, width), routes.T, z, columns * planes, cap, planes, sends[-1]
    )
    slots = lax.all_to_all(outgoing.reshape(sectors, -1, width), "sector", 0, 0, tiled=True)
    shared = shared_expert(normed, shared_gate, shared_up, shared_down, z, planes)
    shared_parts = [shared[0]] + [
        lax.ppermute(shared[k], "expert", [(i, (i + k) % planes) for i in range(planes)]) for k in range(1, planes)
    ]
    results = expert(slots.reshape(-1, width), weights, planes, shared[0])
    results = hold(results, *shared_parts[1:])
    part = width // planes
    back = lax.all_to_all(results.reshape(planes * sectors, -1, part), both, 0, 0, tiled=True)
    return combine(position, gates.T, back.reshape(-1, part), shared_parts)


def solution(mesh):
    in_specs = (
        P("sector", None),
        P(),
        P("sector", None),
        P("sector", None),
        P("sector", None, "expert"),
        P("sector", None, "expert"),
        P("sector", "expert", None),
        P(None, "expert"),
        P(None, "expert"),
        P("expert", None),
    )
    out_specs = P("sector", "expert")
    return jax.shard_map(
        per_device, mesh=mesh, in_specs=in_specs, out_specs=out_specs, check_vma=False
    )
```

```python
import functools

import jax
import jax.numpy as jnp
from jax import lax
from jax.experimental import pallas as pl
from jax.experimental.pallas import tpu as pltpu
from jax.sharding import PartitionSpec as P

F32 = jnp.float32
BF16 = jnp.bfloat16
VMEM_LIMIT = 56 * 1024 * 1024


def dot(a, b):
    return jnp.dot(a, b, preferred_element_type=F32)


def swish(gate, up):
    half = 0.5 * gate
    return ((half + half * jnp.tanh(half)) * up).astype(BF16)


def pack_kernel(half, place, gate, up, down, *sends):
    width = gate.shape[1]
    for r, send in enumerate(sends):
        pick = place[0] ^ r
        expert, part = pick // 2, pick % 2
        cols = pl.ds(pl.multiple_of(part * half, half), half)
        send[:width, :] = gate[expert, :, cols]
        send[width : 2 * width, :] = up[expert, :, cols]
        for n in range(width // half):
            send[2 * width + n * half : 2 * width + (n + 1) * half, :] = down[expert, cols, n * half : (n + 1) * half]


def pack(gate, up, down, place):
    _, width, hidden = gate.shape
    half = hidden // 2
    shape = jax.ShapeDtypeStruct((3 * width, half), BF16)
    return pl.pallas_call(
        functools.partial(pack_kernel, half),
        out_shape=[shape] * 4,
        in_specs=[pl.BlockSpec(memory_space=pltpu.SMEM)] + [pl.BlockSpec(memory_space=pltpu.VMEM)] * 3,
        out_specs=[pl.BlockSpec(memory_space=pltpu.VMEM)] * 4,
        compiler_params=pltpu.CompilerParams(vmem_limit_bytes=VMEM_LIMIT),
        cost_estimate=pl.CostEstimate(flops=0, bytes_accessed=6 * gate.size * 2, transcendentals=0),
    )(place, gate, up, down)


def route_kernel(block, cap, stack, plane, tokens, gain, routes, after, outgoing, normed, position, chosen):
    step = pl.program_id(0)
    rows, width = tokens.shape
    experts = chosen.shape[0]
    columns = experts // stack
    per = outgoing.shape[0] // cap

    @pl.when(step == 0)
    def _():
        earlier = (
            lax.broadcasted_iota(jnp.int32, (block, block), 0) < lax.broadcasted_iota(jnp.int32, (block, block), 1)
        ).astype(F32).astype(BF16)
        m = lax.broadcasted_iota(jnp.int32, (experts, block), 0)
        name = (m % columns) * stack + m // columns
        core, turn = cap // 2, cap // 4
        seen = jnp.zeros((experts, 1), F32)
        for b in range(rows // block):
            at = pl.ds(b * block, block)
            first = routes[0:1, at] == name
            second = routes[1:2, at] == name
            named = jnp.where(first | second, 1.0, 0.0).astype(F32)
            rank = dot(named.astype(BF16), earlier) + seen
            chosen[:, at] = jnp.where(first | second, rank, -1.0)
            seen = seen + jnp.sum(named, axis=1, keepdims=True)
            number = rank.astype(jnp.int32)
            slot = m * core + number // core * turn + number % turn + number // turn % 2 * (experts * core)
            slot = slot.astype(F32)
            position[0:1, at] = jnp.max(jnp.where(first, slot, -1.0), axis=0, keepdims=True)
            position[1:2, at] = jnp.max(jnp.where(second, slot, -1.0), axis=0, keepdims=True)
            values = tokens[at, :].astype(F32)
            scale = lax.rsqrt(jnp.mean(values * values, axis=-1, keepdims=True) + 1e-05)
            normed[at, :] = (values * scale * gain[...]).astype(BF16)

    ranks = lax.broadcasted_iota(jnp.int32, (cap, rows), 0).astype(F32)
    start = plane[0] * columns + step * per
    masks = [jnp.where(ranks == chosen[pl.ds(start + i, 1), :], 1.0, 0.0).astype(BF16) for i in range(per)]
    outgoing[...] = dot(jnp.concatenate(masks, axis=0), normed[...]).astype(BF16)


def route(tokens, gain, routes, plane, experts, cap, stack, after):
    rows, width = tokens.shape
    slots = experts // stack * cap
    block, per = 256, 4 * cap
    return pl.pallas_call(
        functools.partial(route_kernel, block, cap, stack),
        grid=(slots // per,),
        out_shape=[
            jax.ShapeDtypeStruct((slots, width), BF16),
            jax.ShapeDtypeStruct((rows, width), BF16),
            jax.ShapeDtypeStruct((2, rows), F32),
        ],
        in_specs=[
            pl.BlockSpec(memory_space=pltpu.SMEM),
            pl.BlockSpec((rows, width), lambda i: (0, 0)),
            pl.BlockSpec((1, width), lambda i: (0, 0)),
            pl.BlockSpec((2, rows), lambda i: (0, 0)),
            pl.BlockSpec(memory_space=pl.ANY),
        ],
        out_specs=[
            pl.BlockSpec((per, width), lambda i: (i, 0)),
            pl.BlockSpec((rows, width), lambda i: (0, 0)),
            pl.BlockSpec((2, rows), lambda i: (0, 0)),
        ],
        scratch_shapes=[pltpu.VMEM((experts, rows), F32)],
        compiler_params=pltpu.CompilerParams(vmem_limit_bytes=VMEM_LIMIT),
        cost_estimate=pl.CostEstimate(
            flops=2 * slots * rows * width, bytes_accessed=6 * rows * width + 2 * slots * width, transcendentals=rows
        ),
    )(plane, tokens, gain, routes, after)


def shared_kernel(plane, normed, gate, up, down, *rest):
    outs, total = rest[:-1], rest[-1]
    x = normed[...]
    total[...] = dot(swish(dot(x, gate[...]), dot(x, up[...])), down[...])
    planes, part = len(outs), outs[0].shape[1]
    for k, out in enumerate(outs):
        target = (plane[0] + k) % planes
        out[...] = total[:, pl.ds(pl.multiple_of(target * part, part), part)].astype(BF16)


def shared_expert(normed, gate, up, down, plane, planes):
    rows, width = normed.shape
    hidden = gate.shape[1]
    block = 512
    part = width // planes
    whole = [pl.BlockSpec(w.shape, lambda i: (0, 0)) for w in (gate, up, down)]
    return pl.pallas_call(
        shared_kernel,
        grid=(rows // block,),
        out_shape=[jax.ShapeDtypeStruct((rows, part), BF16)] * planes,
        in_specs=[pl.BlockSpec(memory_space=pltpu.SMEM), pl.BlockSpec((block, width), lambda i: (i, 0))] + whole,
        out_specs=[pl.BlockSpec((block, part), lambda i: (i, 0))] * planes,
        scratch_shapes=[pltpu.VMEM((block, width), F32)],
        compiler_params=pltpu.CompilerParams(vmem_limit_bytes=VMEM_LIMIT),
        cost_estimate=pl.CostEstimate(
            flops=6 * rows * width * hidden, bytes_accessed=4 * rows * width, transcendentals=rows * hidden
        ),
    )(plane, normed, gate, up, down)


def expert_kernel(turn, slots, *refs):
    weights, (out, x, kept, total, arrived, sems) = refs[:8], refs[-6:]
    rows, width = total.shape
    each = x.shape[1]
    half = kept.shape[2]
    load = pltpu.make_async_copy(slots.at[:, pl.ds(turn * each, each), :], x, arrived)
    load.start()
    copies = [pltpu.make_async_copy(w, kept.at[n], sems.at[n]) for n, w in enumerate(weights)]
    for copy in copies:
        copy.start()
    load.wait()
    rows_in = x[...].reshape(rows, width)
    for n, copy in enumerate(copies):
        copy.wait()
        w = kept.at[n]
        hidden = swish(dot(rows_in, w[:width, :]), dot(rows_in, w[width : 2 * width, :]))
        for c in range(width // half):
            at = pl.ds(c * half, half)
            part = dot(hidden, w[2 * width + c * half : 2 * width + (c + 1) * half, :])
            total[:, at] = part if n == 0 else total[:, at] + part
    part = out.shape[2]
    for q in range(out.shape[0]):
        out[q] = total[:, q * part : (q + 1) * part].astype(BF16)


def expert(slots, weights, planes, turn, after):
    sources, each, width = slots.shape
    each = each // 2
    rows = sources * each
    hidden = sum(w.shape[1] for w in weights)
    anywhere = pl.BlockSpec(memory_space=pl.ANY)
    return pl.pallas_call(
        functools.partial(expert_kernel, turn),
        out_shape=jax.ShapeDtypeStruct((planes, rows, width // planes), BF16),
        in_specs=[anywhere] * (1 + len(weights) + len(after)),
        out_specs=pl.BlockSpec(memory_space=pltpu.VMEM),
        scratch_shapes=[
            pltpu.VMEM((sources, each, width), BF16),
            pltpu.VMEM((len(weights), *weights[0].shape), BF16),
            pltpu.VMEM((rows, width), F32),
            pltpu.SemaphoreType.DMA,
            pltpu.SemaphoreType.DMA((len(weights),)),
        ],
        compiler_params=pltpu.CompilerParams(vmem_limit_bytes=VMEM_LIMIT),
        cost_estimate=pl.CostEstimate(
            flops=6 * rows * width * hidden, bytes_accessed=4 * rows * width + 6 * width * hidden,
            transcendentals=rows * hidden,
        ),
    )(slots, *weights, *after)


def hold_kernel(*refs):
    pass


def hold(array, *others, flops=0):
    anywhere = pl.BlockSpec(memory_space=pl.ANY)
    return pl.pallas_call(
        hold_kernel,
        out_shape=jax.ShapeDtypeStruct(array.shape, array.dtype),
        in_specs=[anywhere] * (1 + len(others)),
        out_specs=anywhere,
        input_output_aliases={0: 0},
        cost_estimate=pl.CostEstimate(flops=flops, bytes_accessed=0, transcendentals=0),
    )(array, *others)


def combine_kernel(base, position, gates, back, *refs):
    addends, (out, place, gate, total) = refs[:-4], refs[-4:]
    step = pl.program_id(0)
    chunk = back.shape[0]
    rows = out.shape[0]
    block = 512

    @pl.when(step == 0)
    def _():
        for b in range(rows // block):
            at = pl.ds(b * block, block)
            columns = jnp.concatenate([position[:, at], gates[:, at], jnp.zeros((4, block), F32)], axis=0).T
            for n in range(2):
                place[n, at, :] = jnp.broadcast_to(columns[:, n : n + 1], (block, 128)).astype(jnp.int32).astype(jnp.int16)
                gate[n, at, :] = jnp.broadcast_to(columns[:, n + 2 : n + 3], (block, 128)).astype(BF16)
            total[at, :] = sum(part[at, :].astype(F32) for part in addends)

    lane = lax.broadcasted_iota(jnp.int32, (16, 128), 1) + (step * chunk + base)
    numbers = [
        jnp.broadcast_to((lane + j * 128).astype(jnp.int16)[None], (block // 16, 16, 128)).reshape(block, 128)
        for j in range(chunk // 128)
    ]
    for b in range(rows // block):
        at = pl.ds(b * block, block)
        first, second, one, two = place[0, at, :], place[1, at, :], gate[0, at, :], gate[1, at, :]
        weight = [
            jnp.where(number == first, one, jnp.where(number == second, two, jnp.zeros((), BF16))) for number in numbers
        ]
        total[at, :] += dot(jnp.concatenate(weight, axis=1), back[...])

    @pl.when(step == pl.num_programs(0) - 1)
    def _():
        out[...] = total[...].astype(out.dtype)


def combine(position, gates, back, addends, base, kind):
    rows, part = addends[0].shape
    slots = back.shape[0]
    chunk = 1024
    return pl.pallas_call(
        functools.partial(combine_kernel, base),
        grid=(slots // chunk,),
        out_shape=jax.ShapeDtypeStruct((rows, part), kind),
        in_specs=[
            pl.BlockSpec((2, rows), lambda i: (0, 0)),
            pl.BlockSpec((2, rows), lambda i: (0, 0)),
            pl.BlockSpec((chunk, part), lambda i: (i, 0)),
        ]
        + [pl.BlockSpec((rows, part), lambda i: (0, 0))] * len(addends),
        out_specs=pl.BlockSpec((rows, part), lambda i: (0, 0)),
        scratch_shapes=[
            pltpu.VMEM((2, rows, 128), jnp.int16),
            pltpu.VMEM((2, rows, 128), BF16),
            pltpu.VMEM((rows, part), F32),
        ],
        compiler_params=pltpu.CompilerParams(vmem_limit_bytes=VMEM_LIMIT),
        cost_estimate=pl.CostEstimate(
            flops=2 * rows * slots * part, bytes_accessed=10 * rows * part + 2 * slots * part, transcendentals=0
        ),
    )(position, gates, back, *addends)


def per_device(
    tokens,
    norm_gain,
    routes,
    gates,
    expert_gate,
    expert_up,
    expert_down,
    shared_gate,
    shared_up,
    shared_down,
):
    rows, width = tokens.shape
    planes, sectors = lax.axis_size("expert"), lax.axis_size("sector")
    columns = sectors // 2
    cap = 128
    both = ("expert", "sector")
    z = lax.axis_index("expert").astype(jnp.int32).reshape(1)

    sends = pack(expert_gate, expert_up, expert_down, z)
    halves = []
    for r, send in enumerate(sends):
        moves = []
        for source in range(planes):
            for s in range(sectors):
                pick = source ^ r
                target = 2 * (s % 2) + pick // 2
                moves.append((source * sectors + s, target * sectors + (s // 2) * 2 + pick % 2))
        halves.append(lax.ppermute(send, both, moves))

    outgoing, normed, position = route(
        tokens, norm_gain.reshape(1, width), routes.T, z, columns * planes, cap, planes, sends[-1]
    )
    slots = lax.all_to_all(outgoing.reshape(sectors, -1, width), "sector", 0, 0, tiled=True)
    shared = list(shared_expert(normed, shared_gate, shared_up, shared_down, z, planes))
    shared[1] = hold(shared[1], *halves, flops=10**10)
    shared_parts = [shared[0]] + [
        lax.ppermute(shared[k], "expert", [(i, (i + k) % planes) for i in range(planes)]) for k in range(1, planes)
    ]
    halves[0] = hold(halves[0], shared[0])
    weights = halves + [lax.ppermute(half, "sector", [(s, s ^ 1) for s in range(sectors)]) for half in halves]

    part = width // planes
    gates = gates.T
    first = expert(slots, weights, planes, 0, shared[1:])
    first = lax.all_to_all(first.reshape(planes * sectors, -1, part), both, 0, 0, tiled=True).reshape(-1, part)
    second = expert(slots, weights, planes, 1, shared_parts[1:])
    second = lax.all_to_all(second.reshape(planes * sectors, -1, part), both, 0, 0, tiled=True).reshape(-1, part)
    mixed = combine(position, gates, first, shared_parts, 0, F32)
    return combine(position, gates, second, [mixed], first.shape[0], BF16)


def solution(mesh):
    in_specs = (
        P("sector", None),
        P(),
        P("sector", None),
        P("sector", None),
        P("sector", None, "expert"),
        P("sector", None, "expert"),
        P("sector", "expert", None),
        P(None, "expert"),
        P(None, "expert"),
        P("expert", None),
    )
    out_specs = P("sector", "expert")
    return jax.shard_map(
        per_device, mesh=mesh, in_specs=in_specs, out_specs=out_specs, check_vma=False
    )
```

```python
import functools

import jax
import jax.numpy as jnp
from jax import lax
from jax.experimental import pallas as pl
from jax.experimental.pallas import tpu as pltpu
from jax.sharding import PartitionSpec as P

F32 = jnp.float32
BF16 = jnp.bfloat16
VMEM_LIMIT = 56 * 1024 * 1024


def dot(a, b):
    return jnp.dot(a, b, preferred_element_type=F32)


def swish(gate, up):
    half = 0.5 * gate
    return ((half + half * jnp.tanh(half)) * up).astype(BF16)


def pack_kernel(half, place, gate, up, down, *sends):
    width = gate.shape[1]
    for r, send in enumerate(sends):
        pick = place[0] ^ r
        expert, part = pick // 2, pick % 2
        cols = pl.ds(pl.multiple_of(part * half, half), half)
        send[:width, :] = gate[expert, :, cols]
        send[width : 2 * width, :] = up[expert, :, cols]
        for n in range(width // half):
            send[2 * width + n * half : 2 * width + (n + 1) * half, :] = down[expert, cols, n * half : (n + 1) * half]


def pack(gate, up, down, place):
    _, width, hidden = gate.shape
    half = hidden // 2
    shape = jax.ShapeDtypeStruct((3 * width, half), BF16)
    return pl.pallas_call(
        functools.partial(pack_kernel, half),
        out_shape=[shape] * 4,
        in_specs=[pl.BlockSpec(memory_space=pltpu.SMEM)] + [pl.BlockSpec(memory_space=pltpu.VMEM)] * 3,
        out_specs=[pl.BlockSpec(memory_space=pltpu.VMEM)] * 4,
        compiler_params=pltpu.CompilerParams(vmem_limit_bytes=VMEM_LIMIT),
        cost_estimate=pl.CostEstimate(flops=0, bytes_accessed=6 * gate.size * 2, transcendentals=0),
    )(place, gate, up, down)


def route_kernel(block, cap, stack, plane, tokens, gain, routes, after, outgoing, normed, position, chosen):
    step = pl.program_id(0)
    rows, width = tokens.shape
    experts = chosen.shape[0]
    columns = experts // stack
    per = outgoing.shape[0] // cap

    @pl.when(step == 0)
    def _():
        earlier = (
            lax.broadcasted_iota(jnp.int32, (block, block), 0) < lax.broadcasted_iota(jnp.int32, (block, block), 1)
        ).astype(F32).astype(BF16)
        m = lax.broadcasted_iota(jnp.int32, (experts, block), 0)
        name = (m % columns) * stack + m // columns
        core, turn = cap // 2, cap // 4
        seen = jnp.zeros((experts, 1), F32)
        for b in range(rows // block):
            at = pl.ds(b * block, block)
            first = routes[0:1, at] == name
            second = routes[1:2, at] == name
            named = jnp.where(first | second, 1.0, 0.0).astype(F32)
            rank = dot(named.astype(BF16), earlier) + seen
            chosen[:, at] = jnp.where(first | second, rank, -1.0)
            seen = seen + jnp.sum(named, axis=1, keepdims=True)
            number = rank.astype(jnp.int32)
            slot = m * core + number // core * turn + number % turn + number // turn % 2 * (experts * core)
            slot = slot.astype(F32)
            position[0:1, at] = jnp.max(jnp.where(first, slot, -1.0), axis=0, keepdims=True)
            position[1:2, at] = jnp.max(jnp.where(second, slot, -1.0), axis=0, keepdims=True)
            values = tokens[at, :].astype(F32)
            scale = lax.rsqrt(jnp.mean(values * values, axis=-1, keepdims=True) + 1e-05)
            normed[at, :] = (values * scale * gain[...]).astype(BF16)

    ranks = lax.broadcasted_iota(jnp.int32, (cap, rows), 0).astype(F32)
    start = plane[0] * columns + step * per
    masks = [jnp.where(ranks == chosen[pl.ds(start + i, 1), :], 1.0, 0.0).astype(BF16) for i in range(per)]
    outgoing[...] = dot(jnp.concatenate(masks, axis=0), normed[...]).astype(BF16)


def route(tokens, gain, routes, plane, experts, cap, stack, after):
    rows, width = tokens.shape
    slots = experts // stack * cap
    block, per = 256, 4 * cap
    return pl.pallas_call(
        functools.partial(route_kernel, block, cap, stack),
        grid=(slots // per,),
        out_shape=[
            jax.ShapeDtypeStruct((slots, width), BF16),
            jax.ShapeDtypeStruct((rows, width), BF16),
            jax.ShapeDtypeStruct((2, rows), F32),
        ],
        in_specs=[
            pl.BlockSpec(memory_space=pltpu.SMEM),
            pl.BlockSpec((rows, width), lambda i: (0, 0)),
            pl.BlockSpec((1, width), lambda i: (0, 0)),
            pl.BlockSpec((2, rows), lambda i: (0, 0)),
            pl.BlockSpec(memory_space=pl.ANY),
        ],
        out_specs=[
            pl.BlockSpec((per, width), lambda i: (i, 0)),
            pl.BlockSpec((rows, width), lambda i: (0, 0)),
            pl.BlockSpec((2, rows), lambda i: (0, 0)),
        ],
        scratch_shapes=[pltpu.VMEM((experts, rows), F32)],
        compiler_params=pltpu.CompilerParams(vmem_limit_bytes=VMEM_LIMIT),
        cost_estimate=pl.CostEstimate(
            flops=2 * slots * rows * width, bytes_accessed=6 * rows * width + 2 * slots * width, transcendentals=rows
        ),
    )(plane, tokens, gain, routes, after)


def shared_kernel(plane, normed, gate, up, down, *rest):
    outs, total = rest[:-1], rest[-1]
    x = normed[...]
    total[...] = dot(swish(dot(x, gate[...]), dot(x, up[...])), down[...])
    planes, part = len(outs), outs[0].shape[1]
    for k, out in enumerate(outs):
        target = (plane[0] + k) % planes
        out[...] = total[:, pl.ds(pl.multiple_of(target * part, part), part)].astype(BF16)


def shared_expert(normed, gate, up, down, plane, planes):
    rows, width = normed.shape
    hidden = gate.shape[1]
    block = 512
    part = width // planes
    whole = [pl.BlockSpec(w.shape, lambda i: (0, 0)) for w in (gate, up, down)]
    return pl.pallas_call(
        shared_kernel,
        grid=(rows // block,),
        out_shape=[jax.ShapeDtypeStruct((rows, part), BF16)] * planes,
        in_specs=[pl.BlockSpec(memory_space=pltpu.SMEM), pl.BlockSpec((block, width), lambda i: (i, 0))] + whole,
        out_specs=[pl.BlockSpec((block, part), lambda i: (i, 0))] * planes,
        scratch_shapes=[pltpu.VMEM((block, width), F32)],
        compiler_params=pltpu.CompilerParams(vmem_limit_bytes=VMEM_LIMIT),
        cost_estimate=pl.CostEstimate(
            flops=60 * rows * width * hidden, bytes_accessed=4 * rows * width, transcendentals=rows * hidden
        ),
    )(plane, normed, gate, up, down)


def expert_kernel(turn, slots, *refs):
    weights, (out, x, kept, total, arrived, sems) = refs[:8], refs[-6:]
    rows, width = total.shape
    each = x.shape[1]
    half = kept.shape[2]
    load = pltpu.make_async_copy(slots.at[:, pl.ds(turn * each, each), :], x, arrived)
    load.start()
    copies = [pltpu.make_async_copy(w, kept.at[n], sems.at[n]) for n, w in enumerate(weights)]
    for copy in copies:
        copy.start()
    load.wait()
    rows_in = x[...].reshape(rows, width)
    for n, copy in enumerate(copies):
        copy.wait()
        w = kept.at[n]
        hidden = swish(dot(rows_in, w[:width, :]), dot(rows_in, w[width : 2 * width, :]))
        for c in range(width // half):
            at = pl.ds(c * half, half)
            part = dot(hidden, w[2 * width + c * half : 2 * width + (c + 1) * half, :])
            total[:, at] = part if n == 0 else total[:, at] + part
    part = out.shape[2]
    for q in range(out.shape[0]):
        out[q] = total[:, q * part : (q + 1) * part].astype(BF16)


def expert(slots, weights, planes, turn, after):
    sources, each, width = slots.shape
    each = each // 2
    rows = sources * each
    hidden = sum(w.shape[1] for w in weights)
    anywhere = pl.BlockSpec(memory_space=pl.ANY)
    return pl.pallas_call(
        functools.partial(expert_kernel, turn),
        out_shape=jax.ShapeDtypeStruct((planes, rows, width // planes), BF16),
        in_specs=[anywhere] * (1 + len(weights) + len(after)),
        out_specs=pl.BlockSpec(memory_space=pltpu.VMEM),
        scratch_shapes=[
            pltpu.VMEM((sources, each, width), BF16),
            pltpu.VMEM((len(weights), *weights[0].shape), BF16),
            pltpu.VMEM((rows, width), F32),
            pltpu.SemaphoreType.DMA,
            pltpu.SemaphoreType.DMA((len(weights),)),
        ],
        compiler_params=pltpu.CompilerParams(vmem_limit_bytes=VMEM_LIMIT),
        cost_estimate=pl.CostEstimate(
            flops=6 * rows * width * hidden, bytes_accessed=4 * rows * width + 6 * width * hidden,
            transcendentals=rows * hidden,
        ),
    )(slots, *weights, *after)


def hold_kernel(*refs):
    pass


def hold(array, *others):
    anywhere = pl.BlockSpec(memory_space=pl.ANY)
    return pl.pallas_call(
        hold_kernel,
        out_shape=jax.ShapeDtypeStruct(array.shape, array.dtype),
        in_specs=[anywhere] * (1 + len(others)),
        out_specs=anywhere,
        input_output_aliases={0: 0},
    )(array, *others)


def combine_kernel(base, position, gates, back, *refs):
    addends, out = refs[:-1], refs[-1]
    rows, slots = out.shape[0], back.shape[0]
    block, chunk = 512, 1024
    lane = lax.broadcasted_iota(jnp.int32, (16, 128), 1) + base

    def wide(column):
        return jnp.broadcast_to(column, (block, 128))

    for b in range(rows // block):
        at = pl.ds(b * block, block)
        columns = jnp.concatenate([position[:, at], gates[:, at], jnp.zeros((4, block), F32)], axis=0).T
        first, second = [wide(columns[:, n : n + 1]).astype(jnp.int32).astype(jnp.int16) for n in (0, 1)]
        one, two = [wide(columns[:, n : n + 1]).astype(BF16) for n in (2, 3)]
        total = sum(part[at, :].astype(F32) for part in addends)
        for c in range(0, slots, chunk):
            weight = []
            for j in range(c, c + chunk, 128):
                number = (lane + j).astype(jnp.int16)[None]
                number = jnp.broadcast_to(number, (block // 16, 16, 128)).reshape(block, 128)
                weight.append(jnp.where(number == first, one, jnp.where(number == second, two, jnp.zeros((), BF16))))
            total = total + dot(jnp.concatenate(weight, axis=1), back[c : c + chunk, :])
        out[at, :] = total.astype(out.dtype)


def combine(position, gates, back, addends, base, kind):
    rows, part = addends[0].shape
    slots = back.shape[0]
    return pl.pallas_call(
        functools.partial(combine_kernel, base),
        out_shape=jax.ShapeDtypeStruct((rows, part), kind),
        in_specs=[pl.BlockSpec(memory_space=pltpu.VMEM)] * (3 + len(addends)),
        out_specs=pl.BlockSpec(memory_space=pltpu.VMEM),
        compiler_params=pltpu.CompilerParams(vmem_limit_bytes=40 * 1024 * 1024),
        cost_estimate=pl.CostEstimate(
            flops=2 * rows * slots * part, bytes_accessed=10 * rows * part + 2 * slots * part, transcendentals=0
        ),
    )(position, gates, back, *addends)


def per_device(
    tokens,
    norm_gain,
    routes,
    gates,
    expert_gate,
    expert_up,
    expert_down,
    shared_gate,
    shared_up,
    shared_down,
):
    rows, width = tokens.shape
    planes, sectors = lax.axis_size("expert"), lax.axis_size("sector")
    columns = sectors // 2
    cap = 128
    both = ("expert", "sector")
    z = lax.axis_index("expert").astype(jnp.int32).reshape(1)

    sends = pack(expert_gate, expert_up, expert_down, z)
    halves = []
    for r, send in enumerate(sends):
        moves = []
        for source in range(planes):
            for s in range(sectors):
                pick = source ^ r
                target = 2 * (s % 2) + pick // 2
                moves.append((source * sectors + s, target * sectors + (s // 2) * 2 + pick % 2))
        halves.append(lax.ppermute(send, both, moves))

    outgoing, normed, position = route(
        tokens, norm_gain.reshape(1, width), routes.T, z, columns * planes, cap, planes, sends[-1]
    )
    slots = lax.all_to_all(outgoing.reshape(sectors, -1, width), "sector", 0, 0, tiled=True)
    shared = shared_expert(normed, shared_gate, shared_up, shared_down, z, planes)
    shared_parts = [shared[0]] + [
        lax.ppermute(shared[k], "expert", [(i, (i + k) % planes) for i in range(planes)]) for k in range(1, planes)
    ]
    halves[0] = hold(halves[0], shared[0])
    weights = halves + [lax.ppermute(half, "sector", [(s, s ^ 1) for s in range(sectors)]) for half in halves]

    part = width // planes
    gates = gates.T
    first = expert(slots, weights, planes, 0, shared[1:])
    first = lax.all_to_all(first.reshape(planes * sectors, -1, part), both, 0, 0, tiled=True).reshape(-1, part)
    second = expert(slots, weights, planes, 1, shared_parts[1:])
    second = lax.all_to_all(second.reshape(planes * sectors, -1, part), both, 0, 0, tiled=True).reshape(-1, part)
    mixed = combine(position, gates, first, shared_parts, 0, F32)
    return combine(position, gates, second, [mixed], first.shape[0], BF16)


def solution(mesh):
    in_specs = (
        P("sector", None),
        P(),
        P("sector", None),
        P("sector", None),
        P("sector", None, "expert"),
        P("sector", None, "expert"),
        P("sector", "expert", None),
        P(None, "expert"),
        P(None, "expert"),
        P("expert", None),
    )
    out_specs = P("sector", "expert")
    return jax.shard_map(
        per_device, mesh=mesh, in_specs=in_specs, out_specs=out_specs, check_vma=False
    )
```

```python
import functools

import jax
import jax.numpy as jnp
from jax import lax
from jax.experimental import pallas as pl
from jax.experimental.pallas import tpu as pltpu
from jax.sharding import PartitionSpec as P

F32 = jnp.float32
BF16 = jnp.bfloat16
VMEM_LIMIT = 56 * 1024 * 1024


def dot(a, b):
    return jnp.dot(a, b, preferred_element_type=F32)


def swish(gate, up):
    half = 0.5 * gate
    return ((half + half * jnp.tanh(half)) * up).astype(BF16)


def pack_kernel(half, place, gate, up, down, *sends):
    width = gate.shape[1]
    for r, send in enumerate(sends):
        pick = place[0] ^ r
        expert, part = pick // 2, pick % 2
        cols = pl.ds(pl.multiple_of(part * half, half), half)
        send[:width, :] = gate[expert, :, cols]
        send[width : 2 * width, :] = up[expert, :, cols]
        for n in range(width // half):
            send[2 * width + n * half : 2 * width + (n + 1) * half, :] = down[expert, cols, n * half : (n + 1) * half]


def pack(gate, up, down, place):
    _, width, hidden = gate.shape
    half = hidden // 2
    shape = jax.ShapeDtypeStruct((3 * width, half), BF16)
    return pl.pallas_call(
        functools.partial(pack_kernel, half),
        out_shape=[shape] * 4,
        in_specs=[pl.BlockSpec(memory_space=pltpu.SMEM)] + [pl.BlockSpec(memory_space=pltpu.VMEM)] * 3,
        out_specs=[pl.BlockSpec(memory_space=pltpu.VMEM)] * 4,
        compiler_params=pltpu.CompilerParams(vmem_limit_bytes=VMEM_LIMIT),
        cost_estimate=pl.CostEstimate(flops=0, bytes_accessed=6 * gate.size * 2, transcendentals=0),
    )(place, gate, up, down)


def route_kernel(block, cap, stack, plane, tokens, gain, routes, after, outgoing, normed, position, chosen):
    step = pl.program_id(0)
    rows, width = tokens.shape
    experts = chosen.shape[0]
    columns = experts // stack
    per = outgoing.shape[0] // cap

    @pl.when(step == 0)
    def _():
        earlier = (
            lax.broadcasted_iota(jnp.int32, (block, block), 0) < lax.broadcasted_iota(jnp.int32, (block, block), 1)
        ).astype(F32).astype(BF16)
        m = lax.broadcasted_iota(jnp.int32, (experts, block), 0)
        name = (m % columns) * stack + m // columns
        core, turn = cap // 2, cap // 4
        seen = jnp.zeros((experts, 1), F32)
        for b in range(rows // block):
            at = pl.ds(b * block, block)
            first = routes[0:1, at] == name
            second = routes[1:2, at] == name
            named = jnp.where(first | second, 1.0, 0.0).astype(F32)
            rank = dot(named.astype(BF16), earlier) + seen
            chosen[:, at] = jnp.where(first | second, rank, -1.0)
            seen = seen + jnp.sum(named, axis=1, keepdims=True)
            number = rank.astype(jnp.int32)
            slot = m * core + number // core * turn + number % turn + number // turn % 2 * (experts * core)
            slot = slot.astype(F32)
            position[0:1, at] = jnp.max(jnp.where(first, slot, -1.0), axis=0, keepdims=True)
            position[1:2, at] = jnp.max(jnp.where(second, slot, -1.0), axis=0, keepdims=True)
            values = tokens[at, :].astype(F32)
            scale = lax.rsqrt(jnp.mean(values * values, axis=-1, keepdims=True) + 1e-05)
            normed[at, :] = (values * scale * gain[...]).astype(BF16)

    ranks = lax.broadcasted_iota(jnp.int32, (cap, rows), 0).astype(F32)
    start = plane[0] * columns + step * per
    masks = [jnp.where(ranks == chosen[pl.ds(start + i, 1), :], 1.0, 0.0).astype(BF16) for i in range(per)]
    outgoing[...] = dot(jnp.concatenate(masks, axis=0), normed[...]).astype(BF16)


def route(tokens, gain, routes, plane, experts, cap, stack, after):
    rows, width = tokens.shape
    slots = experts // stack * cap
    block, per = 256, 4 * cap
    return pl.pallas_call(
        functools.partial(route_kernel, block, cap, stack),
        grid=(slots // per,),
        out_shape=[
            jax.ShapeDtypeStruct((slots, width), BF16),
            jax.ShapeDtypeStruct((rows, width), BF16),
            jax.ShapeDtypeStruct((2, rows), F32),
        ],
        in_specs=[
            pl.BlockSpec(memory_space=pltpu.SMEM),
            pl.BlockSpec((rows, width), lambda i: (0, 0)),
            pl.BlockSpec((1, width), lambda i: (0, 0)),
            pl.BlockSpec((2, rows), lambda i: (0, 0)),
            pl.BlockSpec(memory_space=pl.ANY),
        ],
        out_specs=[
            pl.BlockSpec((per, width), lambda i: (i, 0)),
            pl.BlockSpec((rows, width), lambda i: (0, 0)),
            pl.BlockSpec((2, rows), lambda i: (0, 0)),
        ],
        scratch_shapes=[pltpu.VMEM((experts, rows), F32)],
        compiler_params=pltpu.CompilerParams(vmem_limit_bytes=VMEM_LIMIT),
        cost_estimate=pl.CostEstimate(
            flops=2 * slots * rows * width, bytes_accessed=6 * rows * width + 2 * slots * width, transcendentals=rows
        ),
    )(plane, tokens, gain, routes, after)


def shared_kernel(plane, normed, gate, up, down, *rest):
    outs, total = rest[:-1], rest[-1]
    x = normed[...]
    total[...] = dot(swish(dot(x, gate[...]), dot(x, up[...])), down[...])
    planes, part = len(outs), outs[0].shape[1]
    for k, out in enumerate(outs):
        target = (plane[0] + k) % planes
        out[...] = total[:, pl.ds(pl.multiple_of(target * part, part), part)].astype(BF16)


def shared_expert(normed, gate, up, down, plane, planes):
    rows, width = normed.shape
    hidden = gate.shape[1]
    block = 512
    part = width // planes
    whole = [pl.BlockSpec(w.shape, lambda i: (0, 0)) for w in (gate, up, down)]
    return pl.pallas_call(
        shared_kernel,
        grid=(rows // block,),
        out_shape=[jax.ShapeDtypeStruct((rows, part), BF16)] * planes,
        in_specs=[pl.BlockSpec(memory_space=pltpu.SMEM), pl.BlockSpec((block, width), lambda i: (i, 0))] + whole,
        out_specs=[pl.BlockSpec((block, part), lambda i: (i, 0))] * planes,
        scratch_shapes=[pltpu.VMEM((block, width), F32)],
        compiler_params=pltpu.CompilerParams(vmem_limit_bytes=VMEM_LIMIT),
        cost_estimate=pl.CostEstimate(
            flops=60 * rows * width * hidden, bytes_accessed=4 * rows * width, transcendentals=rows * hidden
        ),
    )(plane, normed, gate, up, down)


def expert_kernel(turn, slots, *refs):
    weights, (out, x, kept, total, arrived, sems) = refs[:8], refs[-6:]
    rows, width = total.shape
    each = x.shape[1]
    half = kept.shape[2]
    load = pltpu.make_async_copy(slots.at[:, pl.ds(turn * each, each), :], x, arrived)
    load.start()
    copies = [pltpu.make_async_copy(w, kept.at[n], sems.at[n]) for n, w in enumerate(weights)]
    for copy in copies:
        copy.start()
    load.wait()
    rows_in = x[...].reshape(rows, width)
    for n, copy in enumerate(copies):
        copy.wait()
        w = kept.at[n]
        hidden = swish(dot(rows_in, w[:width, :]), dot(rows_in, w[width : 2 * width, :]))
        for c in range(width // half):
            at = pl.ds(c * half, half)
            part = dot(hidden, w[2 * width + c * half : 2 * width + (c + 1) * half, :])
            total[:, at] = part if n == 0 else total[:, at] + part
    part = out.shape[2]
    for q in range(out.shape[0]):
        out[q] = total[:, q * part : (q + 1) * part].astype(BF16)


def expert(slots, weights, planes, turn, after):
    sources, each, width = slots.shape
    each = each // 2
    rows = sources * each
    hidden = sum(w.shape[1] for w in weights)
    anywhere = pl.BlockSpec(memory_space=pl.ANY)
    return pl.pallas_call(
        functools.partial(expert_kernel, turn),
        out_shape=jax.ShapeDtypeStruct((planes, rows, width // planes), BF16),
        in_specs=[anywhere] * (1 + len(weights) + len(after)),
        out_specs=pl.BlockSpec(memory_space=pltpu.VMEM),
        scratch_shapes=[
            pltpu.VMEM((sources, each, width), BF16),
            pltpu.VMEM((len(weights), *weights[0].shape), BF16),
            pltpu.VMEM((rows, width), F32),
            pltpu.SemaphoreType.DMA,
            pltpu.SemaphoreType.DMA((len(weights),)),
        ],
        compiler_params=pltpu.CompilerParams(vmem_limit_bytes=VMEM_LIMIT),
        cost_estimate=pl.CostEstimate(
            flops=6 * rows * width * hidden, bytes_accessed=4 * rows * width + 6 * width * hidden,
            transcendentals=rows * hidden,
        ),
    )(slots, *weights, *after)


def hold_kernel(*refs):
    pass


def hold(array, *others):
    anywhere = pl.BlockSpec(memory_space=pl.ANY)
    return pl.pallas_call(
        hold_kernel,
        out_shape=jax.ShapeDtypeStruct(array.shape, array.dtype),
        in_specs=[anywhere] * (1 + len(others)),
        out_specs=anywhere,
        input_output_aliases={0: 0},
    )(array, *others)


def combine_kernel(base, position, gates, back, *refs):
    addends, out = refs[:-1], refs[-1]
    rows, slots = out.shape[0], back.shape[0]
    block, chunk = 512, 1024
    lane = lax.broadcasted_iota(jnp.int32, (16, 128), 1) + base

    def wide(column):
        return jnp.broadcast_to(column, (block, 128))

    for b in range(rows // block):
        at = pl.ds(b * block, block)
        columns = jnp.concatenate([position[:, at], gates[:, at], jnp.zeros((4, block), F32)], axis=0).T
        first, second = [wide(columns[:, n : n + 1]).astype(jnp.int32).astype(jnp.int16) for n in (0, 1)]
        one, two = [wide(columns[:, n : n + 1]).astype(BF16) for n in (2, 3)]
        total = sum(part[at, :].astype(F32) for part in addends)
        for c in range(0, slots, chunk):
            weight = []
            for j in range(c, c + chunk, 128):
                number = (lane + j).astype(jnp.int16)[None]
                number = jnp.broadcast_to(number, (block // 16, 16, 128)).reshape(block, 128)
                weight.append(jnp.where(number == first, one, jnp.where(number == second, two, jnp.zeros((), BF16))))
            total = total + dot(jnp.concatenate(weight, axis=1), back[c : c + chunk, :])
        out[at, :] = total.astype(out.dtype)


def combine(position, gates, back, addends, base, kind):
    rows, part = addends[0].shape
    slots = back.shape[0]
    return pl.pallas_call(
        functools.partial(combine_kernel, base),
        out_shape=jax.ShapeDtypeStruct((rows, part), kind),
        in_specs=[pl.BlockSpec(memory_space=pltpu.VMEM)] * (3 + len(addends)),
        out_specs=pl.BlockSpec(memory_space=pltpu.VMEM),
        compiler_params=pltpu.CompilerParams(vmem_limit_bytes=40 * 1024 * 1024),
        cost_estimate=pl.CostEstimate(
            flops=2 * rows * slots * part, bytes_accessed=10 * rows * part + 2 * slots * part, transcendentals=0
        ),
    )(position, gates, back, *addends)


def per_device(
    tokens,
    norm_gain,
    routes,
    gates,
    expert_gate,
    expert_up,
    expert_down,
    shared_gate,
    shared_up,
    shared_down,
):
    rows, width = tokens.shape
    planes, sectors = lax.axis_size("expert"), lax.axis_size("sector")
    columns = sectors // 2
    cap = 128
    both = ("expert", "sector")
    z = lax.axis_index("expert").astype(jnp.int32).reshape(1)

    sends = pack(expert_gate, expert_up, expert_down, z)
    halves = []
    for r, send in enumerate(sends):
        moves = []
        for source in range(planes):
            for s in range(sectors):
                pick = source ^ r
                target = 2 * (s % 2) + pick // 2
                moves.append((source * sectors + s, target * sectors + (s // 2) * 2 + pick % 2))
        halves.append(lax.ppermute(send, both, moves))

    outgoing, normed, position = route(
        tokens, norm_gain.reshape(1, width), routes.T, z, columns * planes, cap, planes, sends[-1]
    )
    slots = lax.all_to_all(outgoing.reshape(sectors, -1, width), "sector", 0, 0, tiled=True)
    shared = shared_expert(normed, shared_gate, shared_up, shared_down, z, planes)
    shared_parts = [shared[0]] + [
        lax.ppermute(shared[k], "expert", [(i, (i + k) % planes) for i in range(planes)]) for k in range(1, planes)
    ]
    halves[0] = hold(halves[0], shared[0])
    weights = halves + [lax.ppermute(half, "sector", [(s, s ^ 1) for s in range(sectors)]) for half in halves]

    part = width // planes
    gates = gates.T
    first = expert(slots, weights, planes, 0, ())
    first = lax.all_to_all(first.reshape(planes * sectors, -1, part), both, 0, 0, tiled=True).reshape(-1, part)
    second = expert(slots, weights, planes, 1, shared[1:])
    second = lax.all_to_all(second.reshape(planes * sectors, -1, part), both, 0, 0, tiled=True).reshape(-1, part)
    mixed = combine(position, gates, first, shared_parts[:1], 0, F32)
    return combine(position, gates, second, [mixed] + shared_parts[1:], first.shape[0], BF16)


def solution(mesh):
    in_specs = (
        P("sector", None),
        P(),
        P("sector", None),
        P("sector", None),
        P("sector", None, "expert"),
        P("sector", None, "expert"),
        P("sector", "expert", None),
        P(None, "expert"),
        P(None, "expert"),
        P("expert", None),
    )
    out_specs = P("sector", "expert")
    return jax.shard_map(
        per_device, mesh=mesh, in_specs=in_specs, out_specs=out_specs, check_vma=False
    )
```

```python
import functools

import jax
import jax.numpy as jnp
from jax import lax
from jax.experimental import pallas as pl
from jax.experimental.pallas import tpu as pltpu
from jax.sharding import PartitionSpec as P

F32 = jnp.float32
BF16 = jnp.bfloat16
VMEM_LIMIT = 56 * 1024 * 1024


def dot(a, b):
    return jnp.dot(a, b, preferred_element_type=F32)


def swish(gate, up):
    half = 0.5 * gate
    return ((half + half * jnp.tanh(half)) * up).astype(BF16)


def pack_kernel(half, place, gate, up, down, *sends):
    width = gate.shape[1]
    for r, send in enumerate(sends):
        pick = place[0] ^ r
        expert, part = pick // 2, pick % 2
        cols = pl.ds(pl.multiple_of(part * half, half), half)
        send[:width, :] = gate[expert, :, cols]
        send[width : 2 * width, :] = up[expert, :, cols]
        for n in range(width // half):
            send[2 * width + n * half : 2 * width + (n + 1) * half, :] = down[expert, cols, n * half : (n + 1) * half]


def pack(gate, up, down, place):
    _, width, hidden = gate.shape
    half = hidden // 2
    shape = jax.ShapeDtypeStruct((3 * width, half), BF16)
    return pl.pallas_call(
        functools.partial(pack_kernel, half),
        out_shape=[shape] * 4,
        in_specs=[pl.BlockSpec(memory_space=pltpu.SMEM)] + [pl.BlockSpec(memory_space=pltpu.VMEM)] * 3,
        out_specs=[pl.BlockSpec(memory_space=pltpu.VMEM)] * 4,
        compiler_params=pltpu.CompilerParams(vmem_limit_bytes=VMEM_LIMIT),
        cost_estimate=pl.CostEstimate(flops=0, bytes_accessed=6 * gate.size * 2, transcendentals=0),
    )(place, gate, up, down)


def route_kernel(block, cap, stack, plane, tokens, gain, routes, after, outgoing, normed, position, chosen):
    step = pl.program_id(0)
    rows, width = tokens.shape
    experts = chosen.shape[0]
    columns = experts // stack
    per = outgoing.shape[0] // cap

    @pl.when(step == 0)
    def _():
        earlier = (
            lax.broadcasted_iota(jnp.int32, (block, block), 0) < lax.broadcasted_iota(jnp.int32, (block, block), 1)
        ).astype(F32).astype(BF16)
        m = lax.broadcasted_iota(jnp.int32, (experts, block), 0)
        name = (m % columns) * stack + m // columns
        core, turn = cap // 2, cap // 4
        seen = jnp.zeros((experts, 1), F32)
        for b in range(rows // block):
            at = pl.ds(b * block, block)
            first = routes[0:1, at] == name
            second = routes[1:2, at] == name
            named = jnp.where(first | second, 1.0, 0.0).astype(F32)
            rank = dot(named.astype(BF16), earlier) + seen
            chosen[:, at] = jnp.where(first | second, rank, -1.0)
            seen = seen + jnp.sum(named, axis=1, keepdims=True)
            number = rank.astype(jnp.int32)
            log = turn.bit_length() - 1
            slot = m * core + ((number >> (log + 1)) << log) + (number & (turn - 1))
            slot = slot + ((number >> log) & 1) * (experts * core)
            slot = slot.astype(F32)
            position[0:1, at] = jnp.max(jnp.where(first, slot, -1.0), axis=0, keepdims=True)
            position[1:2, at] = jnp.max(jnp.where(second, slot, -1.0), axis=0, keepdims=True)
            values = tokens[at, :].astype(F32)
            scale = lax.rsqrt(jnp.mean(values * values, axis=-1, keepdims=True) + 1e-05)
            normed[at, :] = (values * scale * gain[...]).astype(BF16)

    ranks = lax.broadcasted_iota(jnp.int32, (cap, rows), 0).astype(jnp.int16)
    start = plane[0] * columns + step * per
    yes, no = jnp.ones((), BF16), jnp.zeros((), BF16)
    masks = []
    for i in range(per):
        own = jnp.broadcast_to(chosen[pl.ds(start + i, 1), :], (16, rows)).astype(jnp.int32).astype(jnp.int16)[None]
        own = jnp.broadcast_to(own, (cap // 16, 16, rows)).reshape(cap, rows)
        masks.append(jnp.where(ranks == own, yes, no))
    outgoing[...] = dot(jnp.concatenate(masks, axis=0), normed[...]).astype(BF16)


def route(tokens, gain, routes, plane, experts, cap, stack, after):
    rows, width = tokens.shape
    slots = experts // stack * cap
    block, per = 256, 4 * cap
    return pl.pallas_call(
        functools.partial(route_kernel, block, cap, stack),
        grid=(slots // per,),
        out_shape=[
            jax.ShapeDtypeStruct((slots, width), BF16),
            jax.ShapeDtypeStruct((rows, width), BF16),
            jax.ShapeDtypeStruct((2, rows), F32),
        ],
        in_specs=[
            pl.BlockSpec(memory_space=pltpu.SMEM),
            pl.BlockSpec((rows, width), lambda i: (0, 0)),
            pl.BlockSpec((1, width), lambda i: (0, 0)),
            pl.BlockSpec((2, rows), lambda i: (0, 0)),
            pl.BlockSpec(memory_space=pl.ANY),
        ],
        out_specs=[
            pl.BlockSpec((per, width), lambda i: (i, 0)),
            pl.BlockSpec((rows, width), lambda i: (0, 0)),
            pl.BlockSpec((2, rows), lambda i: (0, 0)),
        ],
        scratch_shapes=[pltpu.VMEM((experts, rows), F32)],
        compiler_params=pltpu.CompilerParams(vmem_limit_bytes=VMEM_LIMIT),
        cost_estimate=pl.CostEstimate(
            flops=2 * slots * rows * width, bytes_accessed=6 * rows * width + 2 * slots * width, transcendentals=rows
        ),
    )(plane, tokens, gain, routes, after)


def shared_kernel(plane, normed, gate, up, down, *rest):
    outs, total = rest[:-1], rest[-1]
    x = normed[...]
    total[...] = dot(swish(dot(x, gate[...]), dot(x, up[...])), down[...])
    planes, part = len(outs), outs[0].shape[1]
    for k, out in enumerate(outs):
        target = (plane[0] + k) % planes
        out[...] = total[:, pl.ds(pl.multiple_of(target * part, part), part)].astype(BF16)


def shared_expert(normed, gate, up, down, plane, planes):
    rows, width = normed.shape
    hidden = gate.shape[1]
    block = 512
    part = width // planes
    whole = [pl.BlockSpec(w.shape, lambda i: (0, 0)) for w in (gate, up, down)]
    return pl.pallas_call(
        shared_kernel,
        grid=(rows // block,),
        out_shape=[jax.ShapeDtypeStruct((rows, part), BF16)] * planes,
        in_specs=[pl.BlockSpec(memory_space=pltpu.SMEM), pl.BlockSpec((block, width), lambda i: (i, 0))] + whole,
        out_specs=[pl.BlockSpec((block, part), lambda i: (i, 0))] * planes,
        scratch_shapes=[pltpu.VMEM((block, width), F32)],
        compiler_params=pltpu.CompilerParams(vmem_limit_bytes=VMEM_LIMIT),
        cost_estimate=pl.CostEstimate(
            flops=60 * rows * width * hidden, bytes_accessed=4 * rows * width, transcendentals=rows * hidden
        ),
    )(plane, normed, gate, up, down)


def expert_kernel(turn, slots, *refs):
    weights, (out, x, kept, total, arrived, sems) = refs[:8], refs[-6:]
    rows, width = total.shape
    each = x.shape[1]
    half = kept.shape[2]
    load = pltpu.make_async_copy(slots.at[:, pl.ds(turn * each, each), :], x, arrived)
    load.start()
    copies = [pltpu.make_async_copy(w, kept.at[n], sems.at[n]) for n, w in enumerate(weights)]
    for copy in copies:
        copy.start()
    load.wait()
    rows_in = x[...].reshape(rows, width)
    for n, copy in enumerate(copies):
        copy.wait()
        w = kept.at[n]
        hidden = swish(dot(rows_in, w[:width, :]), dot(rows_in, w[width : 2 * width, :]))
        for c in range(width // half):
            at = pl.ds(c * half, half)
            part = dot(hidden, w[2 * width + c * half : 2 * width + (c + 1) * half, :])
            total[:, at] = part if n == 0 else total[:, at] + part
    part = out.shape[2]
    for q in range(out.shape[0]):
        out[q] = total[:, q * part : (q + 1) * part].astype(BF16)


def expert(slots, weights, planes, turn, after):
    sources, each, width = slots.shape
    each = each // 2
    rows = sources * each
    hidden = sum(w.shape[1] for w in weights)
    anywhere = pl.BlockSpec(memory_space=pl.ANY)
    return pl.pallas_call(
        functools.partial(expert_kernel, turn),
        out_shape=jax.ShapeDtypeStruct((planes, rows, width // planes), BF16),
        in_specs=[anywhere] * (1 + len(weights) + len(after)),
        out_specs=pl.BlockSpec(memory_space=pltpu.VMEM),
        scratch_shapes=[
            pltpu.VMEM((sources, each, width), BF16),
            pltpu.VMEM((len(weights), *weights[0].shape), BF16),
            pltpu.VMEM((rows, width), F32),
            pltpu.SemaphoreType.DMA,
            pltpu.SemaphoreType.DMA((len(weights),)),
        ],
        compiler_params=pltpu.CompilerParams(vmem_limit_bytes=VMEM_LIMIT),
        cost_estimate=pl.CostEstimate(
            flops=6 * rows * width * hidden, bytes_accessed=4 * rows * width + 6 * width * hidden,
            transcendentals=rows * hidden,
        ),
    )(slots, *weights, *after)


def hold_kernel(*refs):
    pass


def hold(array, *others):
    anywhere = pl.BlockSpec(memory_space=pl.ANY)
    return pl.pallas_call(
        hold_kernel,
        out_shape=jax.ShapeDtypeStruct(array.shape, array.dtype),
        in_specs=[anywhere] * (1 + len(others)),
        out_specs=anywhere,
        input_output_aliases={0: 0},
    )(array, *others)


def combine_kernel(base, position, gates, back, *refs):
    addends, out = refs[:-1], refs[-1]
    rows, slots = out.shape[0], back.shape[0]
    block, chunk = 512, 1024
    lane = lax.broadcasted_iota(jnp.int32, (16, 128), 1) + base

    def wide(column):
        return jnp.broadcast_to(column, (block, 128))

    for b in range(rows // block):
        at = pl.ds(b * block, block)
        columns = jnp.concatenate([position[:, at], gates[:, at], jnp.zeros((4, block), F32)], axis=0).T
        first, second = [wide(columns[:, n : n + 1]).astype(jnp.int32).astype(jnp.int16) for n in (0, 1)]
        one, two = [wide(columns[:, n : n + 1]).astype(BF16) for n in (2, 3)]
        total = sum(part[at, :].astype(F32) for part in addends)
        for c in range(0, slots, chunk):
            weight = []
            for j in range(c, c + chunk, 128):
                number = (lane + j).astype(jnp.int16)[None]
                number = jnp.broadcast_to(number, (block // 16, 16, 128)).reshape(block, 128)
                weight.append(jnp.where(number == first, one, jnp.where(number == second, two, jnp.zeros((), BF16))))
            total = total + dot(jnp.concatenate(weight, axis=1), back[c : c + chunk, :])
        out[at, :] = total.astype(out.dtype)


def combine(position, gates, back, addends, base, kind):
    rows, part = addends[0].shape
    slots = back.shape[0]
    return pl.pallas_call(
        functools.partial(combine_kernel, base),
        out_shape=jax.ShapeDtypeStruct((rows, part), kind),
        in_specs=[pl.BlockSpec(memory_space=pltpu.VMEM)] * (3 + len(addends)),
        out_specs=pl.BlockSpec(memory_space=pltpu.VMEM),
        compiler_params=pltpu.CompilerParams(vmem_limit_bytes=40 * 1024 * 1024),
        cost_estimate=pl.CostEstimate(
            flops=2 * rows * slots * part, bytes_accessed=10 * rows * part + 2 * slots * part, transcendentals=0
        ),
    )(position, gates, back, *addends)


def per_device(
    tokens,
    norm_gain,
    routes,
    gates,
    expert_gate,
    expert_up,
    expert_down,
    shared_gate,
    shared_up,
    shared_down,
):
    rows, width = tokens.shape
    planes, sectors = lax.axis_size("expert"), lax.axis_size("sector")
    columns = sectors // 2
    cap = 128
    both = ("expert", "sector")
    z = lax.axis_index("expert").astype(jnp.int32).reshape(1)

    sends = pack(expert_gate, expert_up, expert_down, z)
    halves = []
    for r, send in enumerate(sends):
        moves = []
        for source in range(planes):
            for s in range(sectors):
                pick = source ^ r
                target = 2 * (s % 2) + pick // 2
                moves.append((source * sectors + s, target * sectors + (s // 2) * 2 + pick % 2))
        halves.append(lax.ppermute(send, both, moves))

    outgoing, normed, position = route(
        tokens, norm_gain.reshape(1, width), routes.T, z, columns * planes, cap, planes, sends[-1]
    )
    slots = lax.all_to_all(outgoing.reshape(sectors, -1, width), "sector", 0, 0, tiled=True)
    shared = shared_expert(normed, shared_gate, shared_up, shared_down, z, planes)
    shared_parts = [shared[0]] + [
        lax.ppermute(shared[k], "expert", [(i, (i + k) % planes) for i in range(planes)]) for k in range(1, planes)
    ]
    halves[0] = hold(halves[0], shared[0])
    weights = halves + [lax.ppermute(half, "sector", [(s, s ^ 1) for s in range(sectors)]) for half in halves]

    part = width // planes
    gates = gates.T
    first = expert(slots, weights, planes, 0, shared[1:])
    first = lax.all_to_all(first.reshape(planes * sectors, -1, part), both, 0, 0, tiled=True).reshape(-1, part)
    second = expert(slots, weights, planes, 1, shared_parts[1:])
    second = lax.all_to_all(second.reshape(planes * sectors, -1, part), both, 0, 0, tiled=True).reshape(-1, part)
    mixed = combine(position, gates, first, shared_parts, 0, F32)
    return combine(position, gates, second, [mixed], first.shape[0], BF16)


def solution(mesh):
    in_specs = (
        P("sector", None),
        P(),
        P("sector", None),
        P("sector", None),
        P("sector", None, "expert"),
        P("sector", None, "expert"),
        P("sector", "expert", None),
        P(None, "expert"),
        P(None, "expert"),
        P("expert", None),
    )
    out_specs = P("sector", "expert")
    return jax.shard_map(
        per_device, mesh=mesh, in_specs=in_specs, out_specs=out_specs, check_vma=False
    )
```
